32 devices in a mesh: groups: 2 (over y), row: 4 (over x, core), col: 4 (over z).
Axes of the slice: x: 2, y: 2, z: 4, core: 2. Of those that a mesh axis runs over, the one named last changes fastest.
Arguments:
- latents: bfloat16 [2048, 3072], P(('groups', 'col'), 'row'), parts along dimension 0, may hold values from -400 to 400
- modulation: float32 [16, 2, 3072], P('groups', None, 'row'), parts along dimension 0, may hold values from -3 to 3
- sample_of: int32 [2048], P('groups'), parts along dimension 0, may hold values from 0 to 7, never falling along the last dimension, each value on 1 to 256 neighbouring positions
- timestep: int32 [16], P('groups'), parts along dimension 0, may hold values from 0 to 999
- reward: float32 [16], P('groups'), parts along dimension 0, may hold values from -4 to 4
- qkv_cotangent: bfloat16 [2048, 9216], P(('groups', 'row'), 'col'), parts along dimension 0, may hold values from -18 to 18
- mlp_cotangent: bfloat16 [2048, 12288], P(('groups', 'row'), 'col'), parts along dimension 0, may hold values from -18 to 18
- mlp_preact: bfloat16 [2048, 12288], P(('groups', 'row'), 'col'), parts along dimension 0, may hold values from -6 to 6
- w_qkv: bfloat16 [3072, 9216], P('row', 'col'), may hold values from -0.109375 to 0.109375
- w_mlp: bfloat16 [3072, 12288], P('row', 'col'), may hold values from -0.109375 to 0.109375
Outputs:
- latent_input_gradient: bfloat16 [2048, 3072], P(('groups', 'col'), 'row'), parts along dimension 0
- qkv_weight_grad: bfloat16 [6144, 9216], P(('groups', 'row'), 'col'), parts along dimension 0
- mlp_weight_grad: bfloat16 [6144, 12288], P(('groups', 'row'), 'col'), parts along dimension 0
The draws below stay inside these ranges and needn't reach their ends.
There are 2 independent parts, one for each index of `groups`. The reference program is written for one: setup_inputs(seed, part) draws one part's arguments, and reference() takes and returns one part's arrays. A program takes and returns all parts, laid end to end along the dimension named above; an argument that names none is the same for every part. Nothing has to cross between parts.
Inputs may be any that keep to these rules, and one draw needn't show every extreme that they name: sample_of never falls along the tokens; each of the 8 samples has at least one token, and the longest has exactly 256.
All inputs are finite; a program needn't handle non-finite values.
Results may differ from the reference program's by a relative error of at most 0.012.
Values may be sent and summed in bfloat16 or wider, within the bound.
No kernel may reach another device: no remote copies, remote signals or barrier semaphores. Data moves between devices by JAX's collectives and lax.ppermute only.
A program may use at most 128 MiB of HBM per device.

```python
import math
import jax
import jax.numpy as jnp
import numpy as np
from jax import lax

MODEL_WIDTH = 3072
FFM = 12288
QKV = 9216
TOKENS = 1024
SAMPLES = 8
TSTEPS = 1000
N_COL = 4


def draw_latents(key, part):
    key = jax.random.fold_in(key, 11)
    key_noise, key_rows, key_cols = jax.random.split(key, 3)
    noise = jnp.clip(jax.random.normal(key_noise, (TOKENS, MODEL_WIDTH), jnp.float32), -4.0, 4.0)
    row_scale = jnp.exp(jax.random.uniform(key_rows, (TOKENS, 1), jnp.float32) * math.log(10.0))
    ramp = jnp.arange(MODEL_WIDTH, dtype=jnp.float32)[None, :] / (MODEL_WIDTH - 1)
    jitter = jax.random.uniform(key_cols, (1, MODEL_WIDTH), jnp.float32)
    col_scale = jnp.exp(math.log(10.0) * (0.8 * ramp + 0.2 * jitter))
    return (row_scale * col_scale * noise).astype(jnp.bfloat16)


def place_ends(entries, rng, low, largest):
    extent = entries.shape
    index_at = [jax.random.randint(jax.random.fold_in(rng, axis), (), 0, extent[axis]) for axis in range(len(extent))]
    entries = entries.at[tuple(index_at)].set(low)
    longest = extent.index(max(extent))
    index_at[longest] = (index_at[longest] + 1) % extent[longest]
    return entries.at[tuple(index_at)].set(largest)


def shard_levels(rng, shape, pieces, least, top_value):
    gain, own = 1.0, jax.random.fold_in(rng, 6)
    for dim, parts in pieces:
        draws = jnp.exp(jax.random.uniform(jax.random.fold_in(own, dim), (parts,), jnp.float32, least / len(pieces), top_value / len(pieces)))
        gain = gain * jnp.repeat(draws, shape[dim] // parts).reshape([-1 if axis == dim else 1 for axis in range(len(shape))])
    return gain


def split_up(amount, total, limit, slope):
    loads = [(1 << 20) // math.isqrt(standing ** slope) + 1 for standing in range(2, amount + 1)]
    surplus, given = total - limit - (amount - 1), [1] * (amount - 1)
    while surplus > 0:
        free = [i for i in range(amount - 1) if given[i] < limit]
        whole, left = sum([loads[i] for i in free]), surplus
        for i in free:
            extra = min(limit - given[i], max(1, left * loads[i] // whole), surplus)
            given[i] = given[i] + extra
            surplus = surplus - extra
    return np.array([limit] + given)


def uneven(rng, count, total, bound, lean):
    if count == 2:
        one = jax.random.randint(rng, (), max(1, total - bound), min(bound, total - 1) + 1)
        return jnp.stack([one, total - one])
    sizes = jnp.asarray(split_up(count, total, bound, lean), jnp.int32)
    pairs = (count - 1) // 2
    donor, receiver = sizes[1:1 + 2 * pairs:2], sizes[2:2 + 2 * pairs:2]
    slack = jnp.minimum(donor - 1, bound - receiver)
    passed = jax.random.randint(jax.random.fold_in(rng, 1), (pairs,), 0, 1 << 20) % (slack + 1)
    sizes = sizes.at[1:1 + 2 * pairs:2].set(donor - passed).at[2:2 + 2 * pairs:2].set(receiver + passed)
    return sizes[jax.random.permutation(jax.random.fold_in(rng, 2), count)]


def gaussian(rng, shape, deviation, limit, pieces=(), kind=jnp.bfloat16):
    drawn = deviation * jax.random.normal(rng, shape, jnp.float32)
    if pieces:
        drawn = drawn * shard_levels(rng, shape, pieces, -0.22, 0.18)
    return jnp.clip(drawn, -limit, limit).astype(kind)


def setup_inputs(seed: int = 0, part: int = 0) -> dict:
    arg_keys = jax.random.split(jax.random.key(seed), 11)
    part_splits = jax.random.split(jax.random.fold_in(arg_keys[10], part), 11)
    return {
        "latents": draw_latents(jax.random.fold_in(jax.random.fold_in(arg_keys[10], part), 71), part),
        "modulation": gaussian(part_splits[1], (SAMPLES, 2, MODEL_WIDTH), 0.5, 3.0, ((2, 4),), jnp.float32),
        "sample_of": jnp.searchsorted(jnp.cumsum(uneven(part_splits[2], SAMPLES, TOKENS, TOKENS // 4, 1)), jnp.arange(TOKENS), side="right").astype(jnp.int32),
        "timestep": place_ends(jax.random.randint(part_splits[3], (SAMPLES,), 0, TSTEPS), jax.random.fold_in(part_splits[3], 1), 0, TSTEPS - 1).astype(jnp.int32),
        "reward": gaussian(part_splits[4], (SAMPLES,), 1.0, 4.0, (), jnp.float32),
        "qkv_cotangent": gaussian(part_splits[5], (TOKENS, QKV), 3.0, 18.0, ((0, 4), (1, 4))),
        "mlp_cotangent": gaussian(part_splits[6], (TOKENS, FFM), 3.0, 18.0, ((0, 4), (1, 4))),
        "mlp_preact": gaussian(part_splits[7], (TOKENS, FFM), 1.5, 6.0, ((0, 4), (1, 4))),
        "w_qkv": gaussian(arg_keys[8], (MODEL_WIDTH, QKV), MODEL_WIDTH ** -0.5, 0.109375, ((0, 4), (1, 4))),
        "w_mlp": gaussian(arg_keys[9], (MODEL_WIDTH, FFM), MODEL_WIDTH ** -0.5, 0.109375, ((0, 4), (1, 4))),
    }


EPS = 1e-06
ROOT = math.sqrt(2.0 / math.pi)

def gelu_slope(value):
    inner = ROOT * (value + 0.044715 * value * value * value)
    tangent = jnp.tanh(inner)
    return 0.5 * (1.0 + tangent) + 0.5 * value * (1.0 - tangent * tangent) * ROOT * (1.0 + 3.0 * 0.044715 * value * value)

def reference(latents, modulation, sample_of, timestep, reward, qkv_cotangent, mlp_cotangent, mlp_preact, w_qkv, w_mlp):
    sample_ids = jnp.arange(SAMPLES, dtype=jnp.int32)
    onehot = (sample_ids[:, None] == sample_of[None, :]).astype(jnp.float32)
    counts = lax.optimization_barrier(jnp.sum(onehot, axis=1))
    levels = (jnp.arange(TSTEPS, dtype=jnp.float32) + 0.5) / TSTEPS
    table = 0.5 + 1.5 * levels * (2.0 - levels)
    omega_sample = reward * table[timestep] * lax.rsqrt(counts)
    omega = omega_sample[sample_of][:, None]
    grad_q = (qkv_cotangent.astype(jnp.float32) * omega).astype(jnp.bfloat16)
    grad_m = (mlp_cotangent.astype(jnp.float32) * gelu_slope(mlp_preact.astype(jnp.float32)) * omega).astype(jnp.bfloat16)
    input_float_copy = latents.astype(jnp.float32)
    feature_average = lax.optimization_barrier(jnp.sum(input_float_copy, axis=1, keepdims=True)) / MODEL_WIDTH
    var = lax.optimization_barrier(jnp.sum(input_float_copy * input_float_copy, axis=1, keepdims=True)) / MODEL_WIDTH - feature_average * feature_average
    inverse_deviation = lax.rsqrt(var + EPS)
    centered_normalized = (input_float_copy - feature_average) * inverse_deviation
    modulation_offset = modulation[sample_of, 0, :]
    scale_factor = 1.0 + modulation[sample_of, 1, :]
    norm_output = (centered_normalized * scale_factor + modulation_offset).astype(jnp.bfloat16)
    normed32 = norm_output.astype(jnp.float32)
    q_float = grad_q.astype(jnp.float32)
    m_float = grad_m.astype(jnp.float32)
    qkv_weight_grad = jnp.dot(normed32.T, q_float, precision=lax.Precision.HIGHEST).astype(jnp.bfloat16)
    mlp_weight_grad = jnp.dot(normed32.T, m_float, precision=lax.Precision.HIGHEST).astype(jnp.bfloat16)
    width_q = QKV // N_COL
    width_m = FFM // N_COL
    wq_float = w_qkv.astype(jnp.float32)
    wm_float = w_mlp.astype(jnp.float32)

    def add_block(total, block):
        part = jnp.dot(lax.dynamic_slice_in_dim(q_float, block * width_q, width_q, 1), lax.dynamic_slice_in_dim(wq_float, block * width_q, width_q, 1).T, precision=lax.Precision.HIGHEST)
        part = part + jnp.dot(lax.dynamic_slice_in_dim(m_float, block * width_m, width_m, 1), lax.dynamic_slice_in_dim(wm_float, block * width_m, width_m, 1).T, precision=lax.Precision.HIGHEST)
        rounded = lax.optimization_barrier(part.astype(jnp.bfloat16))
        return (total + rounded.astype(jnp.float32), None)
    normed_grad, _ = lax.scan(add_block, jnp.zeros((TOKENS, MODEL_WIDTH), jnp.float32), jnp.arange(N_COL, dtype=jnp.int32))
    incoming_gradient = normed_grad * scale_factor
    first_moment_term = lax.optimization_barrier(jnp.sum(incoming_gradient, axis=1, keepdims=True)) / MODEL_WIDTH
    second_moment_term = lax.optimization_barrier(jnp.sum(incoming_gradient * centered_normalized, axis=1, keepdims=True)) / MODEL_WIDTH
    latent_input_gradient = inverse_deviation * (incoming_gradient - first_moment_term - centered_normalized * second_moment_term)
    return (latent_input_gradient.astype(jnp.bfloat16), qkv_weight_grad, mlp_weight_grad)
```

```python
import functools
import math

import jax
import jax.numpy as jnp
from jax import lax
from jax.experimental import pallas as pl
from jax.experimental.pallas import tpu as pltpu
from jax.sharding import PartitionSpec as P

MODEL_WIDTH = 3072
TSTEPS = 1000


EPS = 1e-06
ROOT = math.sqrt(2.0 / math.pi)
CUBE = 0.044715
VMEM_BYTES = 48 * 2**20

CORE = [(0, 1), (1, 0), (2, 3), (3, 2)]
CHIP = [(0, 2), (2, 0), (1, 3), (3, 1)]
BOTH = [(0, 3), (3, 0), (1, 2), (2, 1)]
PIECES = (64, 64, 64, 64)


def gelu_slope(value):
    inner = ROOT * (value + CUBE * value * value * value)
    tangent = jnp.tanh(inner)
    return 0.5 * (1.0 + tangent) + 0.5 * value * (1.0 - tangent * tangent) * ROOT * (
        1.0 + 3.0 * CUBE * value * value
    )


def over_tokens(left, right):
    return lax.dot_general(
        left, right, (((0,), (0,)), ((), ())), preferred_element_type=jnp.float32
    )


def against_weight(left, right):
    return lax.dot_general(
        left, right, (((1,), (1,)), ((), ())), preferred_element_type=jnp.float32
    )


def lookup(onehot, table):
    return lax.dot_general(
        onehot,
        table,
        (((0,), (0,)), ((), ())),
        precision=lax.Precision.HIGHEST,
        preferred_element_type=jnp.float32,
    )


def sample_weights(onehot, timestep, reward):
    counts = jnp.sum(onehot, axis=1)
    levels = (jnp.arange(TSTEPS, dtype=jnp.float32) + 0.5) / TSTEPS
    table = 0.5 + 1.5 * levels * (2.0 - levels)
    level_hits = (timestep[:, None] == jnp.arange(TSTEPS, dtype=jnp.int32)[None, :]).astype(
        jnp.float32
    )
    step_weight = jnp.sum(level_hits * table[None, :], axis=1)
    return reward * step_weight * lax.rsqrt(counts)


def params(**more):
    return pltpu.CompilerParams(vmem_limit_bytes=VMEM_BYTES, **more)


def rows_of(refs):
    return refs[0][...] if len(refs) == 1 else jnp.concatenate([ref[...] for ref in refs], axis=0)


def back_kernel(counts, steps, cuts, scaled, *refs):
    lefts, at = [], 0
    for count in counts:
        lefts.append(refs[at : at + count])
        at += count
    weights = refs[at : at + len(counts)]
    at += len(counts)
    if scaled:
        omega = refs[at]
        at += 1
    outs, total = refs[at:-1], refs[-1]
    step = pl.program_id(0)

    @pl.when(step == 0)
    def _():
        total[...] = jnp.zeros_like(total)

    low = 0
    for left, weight, amount in zip(lefts, weights, steps):

        @pl.when((step >= low) & (step < low + amount))
        def _(left=left, weight=weight):
            total[...] += against_weight(rows_of(left), weight[...])

        low += amount

    @pl.when(step == low - 1)
    def _():
        for out, spans in zip(outs, cuts):
            place = 0
            for start, size in spans:
                value = total[start : start + size, :]
                if scaled:
                    value = value * omega[start : start + size, :]
                out[place : place + size, :] = value.astype(out.dtype)
                place += size


def back(lefts, weights, cuts, dtype, tile, omega=None):
    width = weights[0].shape[0]
    rows = sum(left.shape[0] for left in lefts[0])
    steps = [weight.shape[1] // tile for weight in weights]
    lows = [sum(steps[:i]) for i in range(len(steps))]

    def at(low, amount):
        return lambda i: (0, jnp.clip(i - low, 0, amount - 1))

    in_specs = []
    for group, low, amount in zip(lefts, lows, steps):
        in_specs += [pl.BlockSpec((left.shape[0], tile), at(low, amount)) for left in group]
    in_specs += [pl.BlockSpec((width, tile), at(low, amount)) for low, amount in zip(lows, steps)]
    operands = [left for group in lefts for left in group] + list(weights)
    if omega is not None:
        in_specs.append(pl.BlockSpec(omega.shape, lambda i: (0, 0)))
        operands.append(omega)
    sizes = [sum(size for _, size in spans) for spans in cuts]
    depth = sum(weight.shape[1] for weight in weights)
    return pl.pallas_call(
        functools.partial(
            back_kernel, [len(group) for group in lefts], steps, cuts, omega is not None
        ),
        grid=(sum(steps),),
        in_specs=in_specs,
        out_specs=[pl.BlockSpec((size, width), lambda i: (0, 0)) for size in sizes],
        out_shape=[jax.ShapeDtypeStruct((size, width), dtype) for size in sizes],
        scratch_shapes=[pltpu.VMEM((rows, width), jnp.float32)],
        compiler_params=params(),
        cost_estimate=pl.CostEstimate(
            flops=2 * rows * width * depth,
            bytes_accessed=2 * depth * (rows + width),
            transcendentals=0,
        ),
    )(*operands)


def piece_kernel(order, first, second, weight, held, local, omega, *rest):
    outs, total, blocks = rest[:4], rest[4], rest[5]
    step = pl.program_id(0)
    size = first.shape[0]

    @pl.when(step == 0)
    def _():
        total[...] = held[...]

    total[...] += against_weight(rows_of([first, second]), weight[...])

    @pl.when(step == pl.num_programs(0) - 1)
    def _():
        far = (total[...] * omega[...]).astype(jnp.bfloat16)
        blocks[0] = local[:size, :]
        blocks[1] = local[size:, :]
        blocks[2] = far[:size, :]
        blocks[3] = far[size:, :]
        for place, out in enumerate(outs):
            out[...] = blocks[order[place]]


def piece(order, first, second, weight, held, local, omega, tile):
    size, depth = first.shape
    width = weight.shape[0]
    whole = lambda i: (0, 0)
    return pl.pallas_call(
        piece_kernel,
        grid=(depth // tile,),
        in_specs=[
            pl.BlockSpec(memory_space=pltpu.SMEM),
            pl.BlockSpec((size, tile), lambda i: (0, i)),
            pl.BlockSpec((size, tile), lambda i: (0, i)),
            pl.BlockSpec((width, tile), lambda i: (0, i)),
            pl.BlockSpec((2 * size, width), whole),
            pl.BlockSpec((2 * size, width), whole),
            pl.BlockSpec((2 * size, 1), whole),
        ],
        out_specs=[pl.BlockSpec((size, width), whole)] * 4,
        out_shape=[jax.ShapeDtypeStruct((size, width), jnp.bfloat16)] * 4,
        scratch_shapes=[
            pltpu.VMEM((2 * size, width), jnp.float32),
            pltpu.VMEM((4, size, width), jnp.bfloat16),
        ],
        compiler_params=params(),
        cost_estimate=pl.CostEstimate(
            flops=4 * size * width * depth,
            bytes_accessed=2 * depth * (2 * size + width),
            transcendentals=0,
        ),
    )(order, first, second, weight, held, local, omega)


def weight_kernel(*refs):
    normed, grads, out = refs[0], refs[1:-1], refs[-1]
    out[...] = over_tokens(normed[...], rows_of(grads)).astype(out.dtype)


def weight_grad(normed, grads, tile):
    tokens, width = normed.shape
    columns = grads[0].shape[1]
    return pl.pallas_call(
        weight_kernel,
        grid=(columns // tile,),
        in_specs=[pl.BlockSpec((tokens, width), lambda i: (0, 0))]
        + [pl.BlockSpec((grad.shape[0], tile), lambda i: (0, i)) for grad in grads],
        out_specs=pl.BlockSpec((width, tile), lambda i: (0, i)),
        out_shape=jax.ShapeDtypeStruct((width, columns), jnp.bfloat16),
        compiler_params=params(),
        cost_estimate=pl.CostEstimate(
            flops=2 * tokens * width * columns,
            bytes_accessed=2 * (tokens * columns + width * columns + tokens * width),
            transcendentals=0,
        ),
    )(normed, *grads)


def row_sum(pair):
    return (
        pair
        + lax.ppermute(pair, "row", CORE)
        + lax.ppermute(pair, "row", CHIP)
        + lax.ppermute(pair, "row", BOTH)
    )


def on_grid(
    latents,
    modulation,
    sample_of,
    timestep,
    reward,
    qkv_cotangent,
    mlp_cotangent,
    mlp_preact,
    w_qkv,
    w_mlp,
):
    row_id = lax.axis_index("row")
    col_id = lax.axis_index("col")
    tok_col, width_row = latents.shape
    tok_row = qkv_cotangent.shape[0]
    samples = reward.shape[0]
    starts = [sum(PIECES[:k]) for k in range(len(PIECES))]

    latents32 = latents.astype(jnp.float32)
    moments = row_sum(
        jnp.stack([jnp.sum(latents32, axis=1), jnp.sum(latents32 * latents32, axis=1)])
    )

    far_q = lax.ppermute(qkv_cotangent, "row", CHIP)
    side_q = lax.ppermute(qkv_cotangent, "row", CORE)

    sample_ids = jnp.arange(samples, dtype=jnp.int32)
    onehot = (sample_ids[:, None] == sample_of[None, :]).astype(jnp.float32)
    omega = lookup(onehot, sample_weights(onehot, timestep, reward)[:, None])
    blocks = omega.reshape(4, tok_row, 1)
    omega_near = jnp.concatenate(
        [lax.dynamic_index_in_dim(blocks, row_id ^ j, keepdims=False) for j in (0, 1)], axis=0
    )
    omega_far = [lax.dynamic_index_in_dim(blocks, row_id ^ j, keepdims=False) for j in (2, 3)]

    own_m = [
        (
            mlp_cotangent[start : start + size].astype(jnp.float32)
            * gelu_slope(mlp_preact[start : start + size].astype(jnp.float32))
        ).astype(jnp.bfloat16)
        for start, size in zip(starts, PIECES)
    ]
    far_m = [lax.ppermute(part, "row", CHIP) for part in own_m]
    side_m = [lax.ppermute(part, "row", CORE) for part in own_m]

    mod_flat = modulation.reshape(samples, 2 * width_row)
    own_onehot = lax.dynamic_slice_in_dim(onehot, col_id * tok_col, tok_col, 1)
    own_mod = lookup(own_onehot, mod_flat)
    offset = own_mod[:, :width_row]
    scale = 1.0 + own_mod[:, width_row:]
    mean = (moments[0] / MODEL_WIDTH)[:, None]
    rstd = lax.rsqrt((moments[1] / MODEL_WIDTH)[:, None] - mean * mean + EPS)
    own_omega = lax.dynamic_slice_in_dim(omega, col_id * tok_col, tok_col, 0)
    normed = (
        ((latents32 - mean) * rstd * scale + offset) * own_omega
    ).astype(jnp.bfloat16)
    pair = jnp.concatenate(
        [normed, lax.ppermute(normed, "col", [(0, 2), (2, 0), (1, 3), (3, 1)])], axis=0
    )
    gathered = jnp.concatenate(
        [pair, lax.ppermute(pair, "col", [(0, 1), (1, 0), (2, 3), (3, 2)])], axis=0
    ).reshape(2, 2, tok_col, width_row)
    normed_all = jnp.concatenate(
        [
            lax.dynamic_slice(
                gathered, (which % 2, which // 2, 0, 0), (1, 1, tok_col, width_row)
            ).reshape(tok_col, width_row)
            for which in ((row_id ^ j) ^ col_id for j in range(4))
        ],
        axis=0,
    )

    near_cuts = [
        [(start, size), (tok_row + start, size)] for start, size in zip(starts, PIECES)
    ]
    near = back(
        [[qkv_cotangent, side_q], own_m + side_m],
        [w_qkv, w_mlp],
        near_cuts,
        jnp.bfloat16,
        768,
        omega_near,
    )
    farside_q = lax.ppermute(far_q, "row", CORE)
    far = back([[far_q, farside_q]], [w_qkv], near_cuts, jnp.float32, 768)
    qkv_total = weight_grad(normed_all, [qkv_cotangent, side_q, far_q, farside_q], 768)

    order = jnp.stack([row_id ^ ((col_id + step) % 4) for step in range(4)])
    farside_m, incoming = [], []
    for k, (start, size) in enumerate(zip(starts, PIECES)):
        farside_m.append(lax.ppermute(far_m[k], "row", CORE))
        piece_omega = jnp.concatenate([part[start : start + size] for part in omega_far], axis=0)
        sends = piece(
            order, far_m[k], farside_m[k], w_mlp, far[k], near[k], piece_omega, 768
        )
        total = sends[0].astype(jnp.float32)
        for step in (1, 2, 3):
            total = total + lax.ppermute(
                sends[step], "col", [(i, (i + step) % 4) for i in range(4)]
            ).astype(jnp.float32)
        incoming.append(total * scale[start : start + size])

    mlp_total = weight_grad(normed_all, own_m + side_m + far_m + farside_m, 768)

    incoming = jnp.concatenate(incoming, axis=0)
    xhat = (latents32 - mean) * rstd
    terms = row_sum(
        jnp.stack([jnp.sum(incoming, axis=1), jnp.sum(incoming * xhat, axis=1)])
    ) / MODEL_WIDTH
    latent_input_gradient = rstd * (
        incoming - terms[0][:, None] - xhat * terms[1][:, None]
    )
    return latent_input_gradient.astype(jnp.bfloat16), qkv_total, mlp_total


def on_device(
    latents,
    modulation,
    sample_of,
    timestep,
    reward,
    qkv_cotangent,
    mlp_cotangent,
    mlp_preact,
    w_qkv,
    w_mlp,
):
    row_id = lax.axis_index("row")
    col_id = lax.axis_index("col")
    tok_col = latents.shape[0]
    tok_row = qkv_cotangent.shape[0]
    width_row = latents.shape[1]
    samples = reward.shape[0]
    sample_ids = jnp.arange(samples, dtype=jnp.int32)
    onehot = (sample_ids[:, None] == sample_of[None, :]).astype(jnp.float32)
    omega_sample = sample_weights(onehot, timestep, reward)
    omega_tokens = lookup(onehot, omega_sample[:, None])[:, 0]
    omega_rows = lax.dynamic_slice_in_dim(omega_tokens, row_id * tok_row, tok_row)[:, None]
    grad_q = (qkv_cotangent.astype(jnp.float32) * omega_rows).astype(jnp.bfloat16)
    grad_m = (
        mlp_cotangent.astype(jnp.float32) * gelu_slope(mlp_preact.astype(jnp.float32)) * omega_rows
    ).astype(jnp.bfloat16)
    mod_flat = modulation.reshape(samples, 2 * width_row)
    input_float_copy = latents.astype(jnp.float32)
    own_onehot = lax.dynamic_slice_in_dim(onehot, col_id * tok_col, tok_col, 1)
    own_mod = lookup(own_onehot, mod_flat)
    sample_offset = own_mod[:, :width_row]
    sample_scale_factor = 1.0 + own_mod[:, width_row:]
    total_sum, total_square = lax.psum(
        (jnp.sum(input_float_copy, axis=1), jnp.sum(input_float_copy * input_float_copy, axis=1)),
        "row",
    )
    feature_average = (total_sum / MODEL_WIDTH)[:, None]
    inverse_deviation = lax.rsqrt(
        (total_square / MODEL_WIDTH)[:, None] - feature_average * feature_average + EPS
    )
    centered_normalized = (input_float_copy - feature_average) * inverse_deviation
    norm_output = (centered_normalized * sample_scale_factor + sample_offset).astype(jnp.bfloat16)
    normed_all = lax.all_gather(norm_output, "col", axis=0, tiled=True)
    all_q, all_m = (
        lax.all_gather(grad_q, "row", axis=0, tiled=True),
        lax.all_gather(grad_m, "row", axis=0, tiled=True),
    )
    qkv_total = over_tokens(normed_all, all_q)
    mlp_total = over_tokens(normed_all, all_m)
    normed_grad = lax.psum_scatter(
        (against_weight(all_q, w_qkv) + against_weight(all_m, w_mlp)).astype(jnp.bfloat16),
        "col",
        scatter_dimension=0,
        tiled=True,
    ).astype(jnp.float32)
    incoming_gradient = normed_grad * sample_scale_factor
    first_moment_term, second_moment_term = lax.psum(
        (
            jnp.sum(incoming_gradient, axis=1),
            jnp.sum(incoming_gradient * centered_normalized, axis=1),
        ),
        "row",
    )
    latent_input_gradient = inverse_deviation * (
        incoming_gradient
        - (first_moment_term / MODEL_WIDTH)[:, None]
        - centered_normalized * (second_moment_term / MODEL_WIDTH)[:, None]
    )
    return (
        latent_input_gradient.astype(jnp.bfloat16),
        qkv_total.astype(jnp.bfloat16),
        mlp_total.astype(jnp.bfloat16),
    )


def solution(mesh):
    in_specs = (
        P(("groups", "col"), "row"),
        P("groups", None, "row"),
        P("groups"),
        P("groups"),
        P("groups"),
        P(("groups", "row"), "col"),
        P(("groups", "row"), "col"),
        P(("groups", "row"), "col"),
        P("row", "col"),
        P("row", "col"),
    )
    out_specs = (
        P(("groups", "col"), "row"),
        P(("groups", "row"), "col"),
        P(("groups", "row"), "col"),
    )
    small = mesh.shape["row"] == 4 and mesh.shape["col"] == 4
    return jax.shard_map(
        on_grid if small else on_device,
        mesh=mesh,
        in_specs=in_specs,
        out_specs=out_specs,
        check_vma=False,
    )
```

```python
import functools
import math

import jax
import jax.numpy as jnp
from jax import lax
from jax.experimental import pallas as pl
from jax.experimental.pallas import tpu as pltpu
from jax.sharding import PartitionSpec as P

MODEL_WIDTH = 3072
TSTEPS = 1000


EPS = 1e-06
ROOT = math.sqrt(2.0 / math.pi)
CUBE = 0.044715
VMEM_BYTES = 48 * 2**20
QUICK = pl.CostEstimate(flops=1, bytes_accessed=1, transcendentals=0)
AHEAD = 2

CORE = [(0, 1), (1, 0), (2, 3), (3, 2)]
CHIP = [(0, 2), (2, 0), (1, 3), (3, 1)]
BOTH = [(0, 3), (3, 0), (1, 2), (2, 1)]
NEXT, SKIP = CORE, CHIP
PIECES = (32, 144, 80)
STARTS = tuple(sum(PIECES[:k]) for k in range(len(PIECES)))
TURNS = ((0, 1), (2,))


def gelu_slope(value):
    inner = ROOT * (value + CUBE * value * value * value)
    tangent = jnp.tanh(inner)
    return 0.5 * (1.0 + tangent) + 0.5 * value * (1.0 - tangent * tangent) * ROOT * (
        1.0 + 3.0 * CUBE * value * value
    )


def over_tokens(left, right):
    return lax.dot_general(
        left, right, (((0,), (0,)), ((), ())), preferred_element_type=jnp.float32
    )


def against_weight(left, right):
    return lax.dot_general(
        left, right, (((1,), (1,)), ((), ())), preferred_element_type=jnp.float32
    )


def lookup(onehot, table):
    return lax.dot_general(
        onehot,
        table,
        (((0,), (0,)), ((), ())),
        precision=lax.Precision.HIGHEST,
        preferred_element_type=jnp.float32,
    )


def sample_weights(onehot, timestep, reward):
    counts = jnp.sum(onehot, axis=1)
    level = (timestep.astype(jnp.float32) + 0.5) / TSTEPS
    return reward * (0.5 + 1.5 * level * (2.0 - level)) * lax.rsqrt(counts)


def params(**more):
    return pltpu.CompilerParams(vmem_limit_bytes=VMEM_BYTES, **more)


def back_kernel(layout, tile, ordered, seeds, holds, *refs):
    refs = list(refs)
    order = refs.pop(0) if ordered else None
    lefts = [[(place, refs.pop(0)) for place in places] for places in layout]
    weights = [refs.pop(0) for _ in layout]
    seed = refs.pop(0) if seeds else None
    del refs[:holds]
    left_sem, weight_sem, seed_sem = refs[-3:]
    left_buf, weight_buf, total = refs[-6:-3]
    outs = refs[:-6]

    first, place = [], 0
    for index, (start, size) in enumerate(seeds):
        first.append(
            pltpu.make_async_copy(
                seed.at[pl.ds(start, size)], total.at[pl.ds(place, size)], seed_sem.at[index]
            )
        )
        place += size
    for copy in first:
        copy.start()
    tiles, column, number = [], 0, 0
    for group, weight in zip(lefts, weights):
        for low in range(0, weight.shape[1], tile):
            span = pl.ds(column, tile)
            copies = [
                pltpu.make_async_copy(
                    weight.at[:, pl.ds(low, tile)], weight_buf.at[:, span], weight_sem.at[column // tile]
                )
            ]
            for place, left in group:
                copies.append(
                    pltpu.make_async_copy(
                        left.at[:, pl.ds(low, tile)],
                        left_buf.at[pl.ds(place, left.shape[0]), span],
                        left_sem.at[number],
                    )
                )
                number += 1
            tiles.append((span, copies))
            column += tile
    start_tiles = lambda low, high: [copy.start() for _, copies in tiles[low:high] for copy in copies]
    start_tiles(0, AHEAD)
    for copy in first:
        copy.wait()
    for index, (span, copies) in enumerate(tiles):
        start_tiles(index + AHEAD, index + AHEAD + 1)
        for copy in copies:
            copy.wait()
        product = against_weight(left_buf[:, span], weight_buf[:, span])
        if index or seeds:
            total[...] += product
        else:
            total[...] = product
    place = 0
    for index, out in enumerate(outs):
        size = out.shape[0]
        if ordered:
            place = pl.multiple_of(order[index] * size, size)
        out[...] = total[pl.ds(place, size), :].astype(out.dtype)
        place += size


def back(groups, weights, sizes, dtype, tile=768, order=None, seed=None, seeds=(), hold=()):
    width = weights[0].shape[0]
    rows = sum(sizes)
    depth = sum(weight.shape[1] for weight in weights)
    layout = [[place for place, _ in group] for group in groups]
    copies = sum(len(group) * (weight.shape[1] // tile) for group, weight in zip(groups, weights))
    operands = [left for group in groups for _, left in group] + list(weights)
    operands += ([] if seed is None else [seed]) + list(hold)
    in_specs = [pl.BlockSpec(memory_space=pl.ANY)] * len(operands)
    for index in range(len(weights)):
        in_specs[sum(map(len, groups)) + index] = pl.BlockSpec(memory_space=pltpu.HBM)
    if order is not None:
        operands.insert(0, order)
        in_specs.insert(0, pl.BlockSpec(memory_space=pltpu.SMEM))
    return pl.pallas_call(
        functools.partial(
            back_kernel, layout, tile, order is not None, seeds, len(hold)
        ),
        in_specs=in_specs,
        out_specs=[pl.BlockSpec(memory_space=pltpu.VMEM)] * len(sizes),
        out_shape=[jax.ShapeDtypeStruct((size, width), dtype) for size in sizes],
        scratch_shapes=[
            pltpu.VMEM((rows, depth), jnp.bfloat16),
            pltpu.VMEM((width, depth), jnp.bfloat16),
            pltpu.VMEM((rows, width), jnp.float32),
            pltpu.SemaphoreType.DMA((copies,)),
            pltpu.SemaphoreType.DMA((depth // tile,)),
            pltpu.SemaphoreType.DMA((max(1, len(seeds)),)),
        ],
        compiler_params=params(),
        cost_estimate=QUICK,
    )(*operands)


def weight_kernel(count, holds, places, *refs):
    parts, grads, (out, normed) = refs[:4], refs[4 : 4 + count], refs[-2:]

    @pl.when(pl.program_id(0) == 0)
    def _():
        for index, part in enumerate(parts):
            size = part.shape[0]
            normed[pl.ds(pl.multiple_of(places[index] * size, size), size), :] = part[...]

    joined = jnp.concatenate([grad[...] for grad in grads], axis=0)
    out[...] = over_tokens(normed[...], joined).astype(out.dtype)


def weight_grad(places, parts, grads, tile=768, low=0, high=None, held=None, hold=()):
    width = parts[0].shape[1]
    tokens = sum(part.shape[0] for part in parts)
    columns = grads[0].shape[1]
    high = columns // tile if high is None else high
    extra = list(hold) + ([] if held is None else [held])
    operands = [places] + list(parts) + list(grads) + extra
    return pl.pallas_call(
        functools.partial(weight_kernel, len(grads), len(extra)),
        grid=(high - low,),
        in_specs=[pl.BlockSpec(memory_space=pltpu.SMEM)]
        + [pl.BlockSpec(part.shape, lambda i: (0, 0)) for part in parts]
        + [pl.BlockSpec((grad.shape[0], tile), lambda i: (0, i + low)) for grad in grads]
        + [pl.BlockSpec(memory_space=pl.ANY)] * len(extra),
        out_specs=pl.BlockSpec((width, tile), lambda i: (0, i + low)),
        out_shape=jax.ShapeDtypeStruct((width, columns), jnp.bfloat16),
        scratch_shapes=[pltpu.VMEM((tokens, width), jnp.bfloat16)],
        input_output_aliases={} if held is None else {len(operands) - 1: 0},
        compiler_params=params(),
        cost_estimate=QUICK,
    )(*operands)


def after(value, *others):
    return lax.optimization_barrier((value, others))[0]


def row_sum(pair):
    return (
        pair
        + lax.ppermute(pair, "row", CORE)
        + lax.ppermute(pair, "row", CHIP)
        + lax.ppermute(pair, "row", BOTH)
    )


def on_grid(
    latents,
    modulation,
    sample_of,
    timestep,
    reward,
    qkv_cotangent,
    mlp_cotangent,
    mlp_preact,
    w_qkv,
    w_mlp,
):
    row_id = lax.axis_index("row")
    col_id = lax.axis_index("col")
    tok_col, width_row = latents.shape
    tok_row = qkv_cotangent.shape[0]
    samples = reward.shape[0]
    own_first = (row_id ^ col_id) % 2
    order = jnp.stack([own_first, 1 - own_first])

    latents32 = latents.astype(jnp.float32)
    moments = row_sum(
        jnp.stack([jnp.sum(latents32, axis=1), jnp.sum(latents32 * latents32, axis=1)])
    )

    far_q = lax.ppermute(qkv_cotangent, "row", CHIP)
    side_q = lax.ppermute(qkv_cotangent, "row", CORE)

    sample_ids = jnp.arange(samples, dtype=jnp.int32)
    onehot = (sample_ids[:, None] == sample_of[None, :]).astype(jnp.float32)
    omega_sample = sample_weights(onehot, timestep, reward)
    own_onehot = lax.dynamic_slice_in_dim(onehot, col_id * tok_col, tok_col, 1)
    own_mod = lookup(own_onehot, modulation.reshape(samples, 2 * width_row))
    own_omega = lookup(own_onehot, omega_sample[:, None])
    offset = own_mod[:, :width_row]
    scale = 1.0 + own_mod[:, width_row:]
    mean = (moments[0] / MODEL_WIDTH)[:, None]
    rstd = lax.rsqrt((moments[1] / MODEL_WIDTH)[:, None] - mean * mean + EPS)
    xhat = (latents32 - mean) * rstd
    normed = ((xhat * scale + offset) * own_omega).astype(jnp.bfloat16)
    scale_omega = scale * own_omega
    across = lax.ppermute(normed, "col", SKIP)
    normed_next = lax.ppermute(normed, "col", NEXT)

    mlp_preact = after(mlp_preact, normed)
    own_m = [
        (
            mlp_cotangent[start : start + size].astype(jnp.float32)
            * gelu_slope(mlp_preact[start : start + size].astype(jnp.float32))
        ).astype(jnp.bfloat16)
        for start, size in zip(STARTS, PIECES)
    ]
    side_m = [lax.ppermute(part, "row", CORE) for part in own_m]
    far_m = [lax.ppermute(part, "row", CHIP) for part in own_m]

    near_keep, near_send = back(
        [
            [(0, qkv_cotangent), (tok_row, side_q)],
            [(start, part) for start, part in zip(STARTS, own_m)]
            + [(tok_row + start, part) for start, part in zip(STARTS, side_m)],
        ],
        [w_qkv, w_mlp],
        [tok_row, tok_row],
        jnp.bfloat16,
        order=order,
        hold=[normed],
    )
    near_next = lax.ppermute(near_send, "col", NEXT)
    across_next = lax.ppermute(after(across, near_send), "col", NEXT)

    places = jnp.stack([row_id ^ col_id ^ j for j in (0, 2, 1, 3)])
    parts = [normed, across, normed_next, across_next]

    farside_q = lax.ppermute(after(far_q, near_send, across, normed_next, far_m[0]), "row", CORE)
    far = back(
        [[(0, far_q), (tok_row, farside_q)]],
        [w_qkv],
        [2 * tok_row],
        jnp.float32,
    )[0]
    near_half = near_keep.astype(jnp.float32) + after(near_next, far).astype(jnp.float32)
    takes_near = row_id // 2 == col_id // 2

    qkv_total = weight_grad(
        places, parts, [qkv_cotangent, side_q, far_q, farside_q], hold=[far]
    )
    farside_m, hold, halves = [], [qkv_total], []
    for turn in TURNS:
        for k in turn:
            farside_m.append(lax.ppermute(after(far_m[k], hold), "row", CORE))
        start, size = STARTS[turn[0]], sum(PIECES[k] for k in turn)
        keep, send = back(
            [
                [(STARTS[k] - start, far_m[k]) for k in turn]
                + [(size + STARTS[k] - start, farside_m[k]) for k in turn]
            ],
            [w_mlp],
            [size, size],
            jnp.bfloat16,
            order=order,
            seed=far,
            seeds=((start, size), (tok_row + start, size)),
            hold=hold,
        )
        hold = [keep]
        halves.append((start, size, keep, lax.ppermute(send, "col", NEXT)))

    all_m = own_m + side_m + far_m + farside_m
    mlp_total = weight_grad(places, parts, all_m, hold=hold)

    incoming = []
    for start, size, keep, send in halves:
        far_half = keep.astype(jnp.float32) + send.astype(jnp.float32)
        near_piece = near_half[start : start + size]
        own = jnp.where(takes_near, near_piece, far_half)
        other = jnp.where(takes_near, far_half, near_piece).astype(jnp.bfloat16)
        arrived = after(lax.ppermute(other, "col", SKIP), mlp_total)
        incoming.append(own + arrived.astype(jnp.float32))
    incoming = jnp.concatenate(incoming, axis=0) * scale_omega
    own_terms = jnp.stack([jnp.sum(incoming, axis=1), jnp.sum(incoming * xhat, axis=1)])
    terms = row_sum(own_terms) / MODEL_WIDTH
    latent_input_gradient = rstd * (
        incoming - terms[0][:, None] - xhat * terms[1][:, None]
    )
    return latent_input_gradient.astype(jnp.bfloat16), qkv_total, mlp_total


def on_device(
    latents,
    modulation,
    sample_of,
    timestep,
    reward,
    qkv_cotangent,
    mlp_cotangent,
    mlp_preact,
    w_qkv,
    w_mlp,
):
    row_id = lax.axis_index("row")
    col_id = lax.axis_index("col")
    tok_col = latents.shape[0]
    tok_row = qkv_cotangent.shape[0]
    width_row = latents.shape[1]
    samples = reward.shape[0]
    sample_ids = jnp.arange(samples, dtype=jnp.int32)
    onehot = (sample_ids[:, None] == sample_of[None, :]).astype(jnp.float32)
    omega_sample = sample_weights(onehot, timestep, reward)
    omega_tokens = lookup(onehot, omega_sample[:, None])[:, 0]
    omega_rows = lax.dynamic_slice_in_dim(omega_tokens, row_id * tok_row, tok_row)[:, None]
    grad_q = (qkv_cotangent.astype(jnp.float32) * omega_rows).astype(jnp.bfloat16)
    grad_m = (
        mlp_cotangent.astype(jnp.float32) * gelu_slope(mlp_preact.astype(jnp.float32)) * omega_rows
    ).astype(jnp.bfloat16)
    mod_flat = modulation.reshape(samples, 2 * width_row)
    input_float_copy = latents.astype(jnp.float32)
    own_onehot = lax.dynamic_slice_in_dim(onehot, col_id * tok_col, tok_col, 1)
    own_mod = lookup(own_onehot, mod_flat)
    sample_offset = own_mod[:, :width_row]
    sample_scale_factor = 1.0 + own_mod[:, width_row:]
    total_sum, total_square = lax.psum(
        (jnp.sum(input_float_copy, axis=1), jnp.sum(input_float_copy * input_float_copy, axis=1)),
        "row",
    )
    feature_average = (total_sum / MODEL_WIDTH)[:, None]
    inverse_deviation = lax.rsqrt(
        (total_square / MODEL_WIDTH)[:, None] - feature_average * feature_average + EPS
    )
    centered_normalized = (input_float_copy - feature_average) * inverse_deviation
    norm_output = (centered_normalized * sample_scale_factor + sample_offset).astype(jnp.bfloat16)
    normed_all = lax.all_gather(norm_output, "col", axis=0, tiled=True)
    all_q, all_m = (
        lax.all_gather(grad_q, "row", axis=0, tiled=True),
        lax.all_gather(grad_m, "row", axis=0, tiled=True),
    )
    qkv_total = over_tokens(normed_all, all_q)
    mlp_total = over_tokens(normed_all, all_m)
    normed_grad = lax.psum_scatter(
        (against_weight(all_q, w_qkv) + against_weight(all_m, w_mlp)).astype(jnp.bfloat16),
        "col",
        scatter_dimension=0,
        tiled=True,
    ).astype(jnp.float32)
    incoming_gradient = normed_grad * sample_scale_factor
    first_moment_term, second_moment_term = lax.psum(
        (
            jnp.sum(incoming_gradient, axis=1),
            jnp.sum(incoming_gradient * centered_normalized, axis=1),
        ),
        "row",
    )
    latent_input_gradient = inverse_deviation * (
        incoming_gradient
        - (first_moment_term / MODEL_WIDTH)[:, None]
        - centered_normalized * (second_moment_term / MODEL_WIDTH)[:, None]
    )
    return (
        latent_input_gradient.astype(jnp.bfloat16),
        qkv_total.astype(jnp.bfloat16),
        mlp_total.astype(jnp.bfloat16),
    )


def solution(mesh):
    in_specs = (
        P(("groups", "col"), "row"),
        P("groups", None, "row"),
        P("groups"),
        P("groups"),
        P("groups"),
        P(("groups", "row"), "col"),
        P(("groups", "row"), "col"),
        P(("groups", "row"), "col"),
        P("row", "col"),
        P("row", "col"),
    )
    out_specs = (
        P(("groups", "col"), "row"),
        P(("groups", "row"), "col"),
        P(("groups", "row"), "col"),
    )
    small = mesh.shape["row"] == 4 and mesh.shape["col"] == 4
    return jax.shard_map(
        on_grid if small else on_device,
        mesh=mesh,
        in_specs=in_specs,
        out_specs=out_specs,
        check_vma=False,
    )
```

```python
import functools
import math

import jax
import jax.numpy as jnp
from jax import lax
from jax.experimental import pallas as pl
from jax.experimental.pallas import tpu as pltpu
from jax.sharding import PartitionSpec as P

MODEL_WIDTH = 3072
TSTEPS = 1000


EPS = 1e-06
ROOT = math.sqrt(2.0 / math.pi)
CUBE = 0.044715
VMEM_BYTES = 36 * 2**20
QUICK = pl.CostEstimate(flops=1, bytes_accessed=1, transcendentals=0)
MARK = jax.ShapeDtypeStruct((8, 128), jnp.float32)
AHEAD = 2

CORE = [(0, 1), (1, 0), (2, 3), (3, 2)]
CHIP = [(0, 2), (2, 0), (1, 3), (3, 1)]
NEXT, SKIP = CORE, CHIP
PIECES = (160, 96)
STARTS = tuple(sum(PIECES[:k]) for k in range(len(PIECES)))
TURNS = ((0,), (1,))
PART = 128


def gelu_slope(value):
    inner = ROOT * (value + CUBE * value * value * value)
    tangent = jnp.tanh(inner)
    return 0.5 * (1.0 + tangent) + 0.5 * value * (1.0 - tangent * tangent) * ROOT * (
        1.0 + 3.0 * CUBE * value * value
    )


def over_tokens(left, right):
    return lax.dot_general(
        left, right, (((0,), (0,)), ((), ())), preferred_element_type=jnp.float32
    )


def against_weight(left, right):
    return lax.dot_general(
        left, right, (((1,), (1,)), ((), ())), preferred_element_type=jnp.float32
    )


def lookup(onehot, table):
    return lax.dot_general(
        onehot,
        table,
        (((0,), (0,)), ((), ())),
        precision=lax.Precision.HIGHEST,
        preferred_element_type=jnp.float32,
    )


def sample_weights(onehot, timestep, reward):
    counts = jnp.sum(onehot, axis=1)
    level = (timestep.astype(jnp.float32) + 0.5) / TSTEPS
    return reward * (0.5 + 1.5 * level * (2.0 - level)) * lax.rsqrt(counts)


def params(**more):
    return pltpu.CompilerParams(vmem_limit_bytes=VMEM_BYTES, **more)


def back_kernel(layout, tile, ordered, seeds, holds, *refs):
    refs = list(refs)
    order = refs.pop(0) if ordered else None
    lefts = [[(place, refs.pop(0)) for place in places] for places in layout]
    weights = [refs.pop(0) for _ in layout]
    seed = refs.pop(0) if seeds else None
    del refs[:holds]
    left_sem, weight_sem, seed_sem = refs[-3:]
    left_buf, weight_buf, total = refs[-6:-3]
    mark, outs = refs[-7], refs[:-7]
    mark[...] = jnp.zeros_like(mark)

    first, place = [], 0
    for index, (start, size) in enumerate(seeds):
        first.append(
            pltpu.make_async_copy(
                seed.at[pl.ds(start, size)], total.at[pl.ds(place, size)], seed_sem.at[index]
            )
        )
        place += size
    for copy in first:
        copy.start()
    tiles, column, number = [], 0, 0
    for group, weight in zip(lefts, weights):
        for low in range(0, weight.shape[1], tile):
            span = pl.ds(column, tile)
            copies = [
                pltpu.make_async_copy(
                    weight.at[:, pl.ds(low, tile)], weight_buf.at[:, span], weight_sem.at[column // tile]
                )
            ]
            for place, left in group:
                copies.append(
                    pltpu.make_async_copy(
                        left.at[:, pl.ds(low, tile)],
                        left_buf.at[pl.ds(place, left.shape[0]), span],
                        left_sem.at[number],
                    )
                )
                number += 1
            tiles.append((span, copies))
            column += tile
    start_tiles = lambda low, high: [copy.start() for _, copies in tiles[low:high] for copy in copies]
    start_tiles(0, AHEAD)
    for copy in first:
        copy.wait()
    for index, (span, copies) in enumerate(tiles):
        start_tiles(index + AHEAD, index + AHEAD + 1)
        for copy in copies:
            copy.wait()
        product = against_weight(left_buf[:, span], weight_buf[:, span])
        if index or seeds:
            total[...] += product
        else:
            total[...] = product
    place = 0
    for index, out in enumerate(outs):
        size = out.shape[0]
        if ordered:
            place = pl.multiple_of(order[index] * size, size)
        out[...] = total[pl.ds(place, size), :].astype(out.dtype)
        place += size


def back(groups, weights, sizes, dtype, tile=768, order=None, seed=None, seeds=(), hold=(), pin=True):
    width = weights[0].shape[0]
    rows = sum(sizes)
    depth = sum(weight.shape[1] for weight in weights)
    layout = [[place for place, _ in group] for group in groups]
    copies = sum(len(group) * (weight.shape[1] // tile) for group, weight in zip(groups, weights))
    operands = [left for group in groups for _, left in group]
    if pin:
        operands = [pltpu.with_memory_space_constraint(left, pltpu.HBM) for left in operands]
    operands += [pltpu.with_memory_space_constraint(weight, pltpu.HBM) for weight in weights]
    if seed is not None:
        operands.append(pltpu.with_memory_space_constraint(seed, pltpu.HBM))
    operands += list(hold)
    in_specs = [pl.BlockSpec(memory_space=pl.ANY)] * len(operands)
    if order is not None:
        operands.insert(0, order)
        in_specs.insert(0, pl.BlockSpec(memory_space=pltpu.SMEM))
    return pl.pallas_call(
        functools.partial(
            back_kernel, layout, tile, order is not None, seeds, len(hold)
        ),
        in_specs=in_specs,
        out_specs=[pl.BlockSpec(memory_space=pltpu.VMEM)] * (len(sizes) + 1),
        out_shape=[
            pltpu.HBM((size, width), dtype) if order is None else jax.ShapeDtypeStruct((size, width), dtype)
            for size in sizes
        ]
        + [MARK],
        scratch_shapes=[
            pltpu.VMEM((rows, depth), jnp.bfloat16),
            pltpu.VMEM((width, depth), jnp.bfloat16),
            pltpu.VMEM((rows, width), jnp.float32),
            pltpu.SemaphoreType.DMA((copies,)),
            pltpu.SemaphoreType.DMA((depth // tile,)),
            pltpu.SemaphoreType.DMA((max(1, len(seeds)),)),
        ],
        compiler_params=params(),
        cost_estimate=QUICK,
    )(*operands)


def weight_kernel(count, holds, places, *refs):
    parts, grads, (out, mark, normed) = refs[:4], refs[4 : 4 + count], refs[-3:]

    @pl.when(pl.program_id(0) == 0)
    def _():
        for index, part in enumerate(parts):
            size = part.shape[0]
            normed[pl.ds(pl.multiple_of(places[index] * size, size), size), :] = part[...]
        mark[...] = jnp.zeros_like(mark)

    joined = jnp.concatenate([grad[...] for grad in grads], axis=0)
    out[...] = over_tokens(normed[...], joined).astype(out.dtype)


def weight_grad(
    places, parts, grads, tile=768, low=0, high=None, held=None, hold=(), pin=True
):
    width = parts[0].shape[1]
    tokens = sum(part.shape[0] for part in parts)
    columns = grads[0].shape[1]
    high = columns // tile if high is None else high
    extra = list(hold) + ([] if held is None else [held])
    arrays = list(parts) + list(grads)
    if pin:
        arrays = [pltpu.with_memory_space_constraint(array, pltpu.HBM) for array in arrays]
    operands = [places] + arrays + extra
    return pl.pallas_call(
        functools.partial(weight_kernel, len(grads), len(extra)),
        grid=(high - low,),
        in_specs=[pl.BlockSpec(memory_space=pltpu.SMEM)]
        + [pl.BlockSpec(part.shape, lambda i: (0, 0)) for part in parts]
        + [pl.BlockSpec((grad.shape[0], tile), lambda i: (0, i + low)) for grad in grads]
        + [pl.BlockSpec(memory_space=pl.ANY)] * len(extra),
        out_specs=[
            pl.BlockSpec((width, tile), lambda i: (0, i + low)),
            pl.BlockSpec(MARK.shape, lambda i: (0, 0)),
        ],
        out_shape=[jax.ShapeDtypeStruct((width, columns), jnp.bfloat16), MARK],
        scratch_shapes=[pltpu.VMEM((tokens, width), jnp.bfloat16)],
        input_output_aliases={} if held is None else {len(operands) - 1: 0},
        compiler_params=params(),
        cost_estimate=QUICK,
    )(*operands)


def after(value, *others):
    return lax.optimization_barrier((value, others))[0]


def row_sum(pair):
    pair += lax.ppermute(pair, "row", CHIP)
    return pair + lax.ppermute(pair, "row", CORE)


def on_grid(
    latents,
    modulation,
    sample_of,
    timestep,
    reward,
    qkv_cotangent,
    mlp_cotangent,
    mlp_preact,
    w_qkv,
    w_mlp,
):
    row_id = lax.axis_index("row")
    col_id = lax.axis_index("col")
    tok_col, width_row = latents.shape
    tok_row = qkv_cotangent.shape[0]
    samples = reward.shape[0]
    own_first = (row_id ^ col_id) % 2
    order = jnp.stack([own_first, 1 - own_first])

    latents32 = latents.astype(jnp.float32)
    moments = jnp.stack([jnp.sum(latents32, axis=1), jnp.sum(latents32 * latents32, axis=1)])
    far_q = lax.ppermute(after(qkv_cotangent, moments), "row", CHIP)
    moments = row_sum(moments)
    side_q = lax.ppermute(qkv_cotangent, "row", CORE)

    sample_ids = jnp.arange(samples, dtype=jnp.int32)
    onehot = (sample_ids[:, None] == sample_of[None, :]).astype(jnp.float32)
    omega_sample = sample_weights(onehot, timestep, reward)
    own_onehot = lax.dynamic_slice_in_dim(onehot, col_id * tok_col, tok_col, 1)
    own_mod = lookup(own_onehot, modulation.reshape(samples, 2 * width_row))
    own_omega = lookup(own_onehot, omega_sample[:, None])
    offset = own_mod[:, :width_row]
    scale = 1.0 + own_mod[:, width_row:]
    mean = (moments[0] / MODEL_WIDTH)[:, None]
    rstd = lax.rsqrt((moments[1] / MODEL_WIDTH)[:, None] - mean * mean + EPS)
    xhat = (latents32 - mean) * rstd
    normed = ((xhat * scale + offset) * own_omega).astype(jnp.bfloat16)
    scale_omega = scale * own_omega
    across = lax.ppermute(normed, "col", SKIP)
    normed_next = lax.ppermute(normed, "col", NEXT)

    mlp_preact = after(mlp_preact, normed)
    own_m = [
        (
            mlp_cotangent[start : start + size].astype(jnp.float32)
            * gelu_slope(mlp_preact[start : start + size].astype(jnp.float32))
        ).astype(jnp.bfloat16)
        for start, size in zip(STARTS, PIECES)
    ]
    side_m = [lax.ppermute(part, "row", CORE) for part in own_m]
    far_m = [lax.ppermute(part, "row", CHIP) for part in own_m]

    near_keep, near_send, mark = back(
        [
            [(0, qkv_cotangent), (tok_row, side_q)],
            [(start, part) for start, part in zip(STARTS, own_m)]
            + [(tok_row + start, part) for start, part in zip(STARTS, side_m)],
        ],
        [w_qkv, w_mlp],
        [tok_row, tok_row],
        jnp.bfloat16,
        order=order,
    )
    near_next = lax.ppermute(near_send, "col", NEXT)

    ready_q = after(far_q, near_send, across, normed_next)
    farside_q = [
        lax.ppermute(ready_q[low : low + PART], "row", CORE) for low in range(0, tok_row, PART)
    ]
    across_next = lax.ppermute(after(across, near_send), "col", NEXT)
    places = jnp.stack([row_id ^ col_id ^ j for j in (0, 2, 1, 3)])
    parts = [normed, across, normed_next, across_next]
    takes_near = row_id // 2 == col_id // 2

    far, mark = back(
        [
            [(0, far_q)]
            + [(tok_row + place * PART, part) for place, part in enumerate(farside_q)]
        ],
        [w_qkv],
        [2 * tok_row],
        jnp.float32,
    )
    q_parts = [qkv_cotangent, side_q, far_q] + farside_q
    qkv_total, mark = weight_grad(places, parts, q_parts, high=1, hold=[mark])
    ready, farside_m, halves = [mark], [], []
    for index, turn in enumerate(TURNS):
        for k in turn:
            farside_m.append(lax.ppermute(after(far_m[k], *ready), "row", CORE))
        start, size = STARTS[turn[0]], sum(PIECES[k] for k in turn)
        keep, send, mark = back(
            [
                [(STARTS[k] - start, far_m[k]) for k in turn]
                + [(size + STARTS[k] - start, farside_m[k]) for k in turn]
            ],
            [w_mlp],
            [size, size],
            jnp.bfloat16,
            order=order,
            seed=far,
            seeds=((start, size), (tok_row + start, size)),
            hold=[mark],
            pin=False,
        )
        send = lax.ppermute(send, "col", NEXT)
        if index == 0:
            qkv_total, mark = weight_grad(
                places, parts, q_parts, low=1, held=qkv_total, hold=[mark]
            )
            ready = [mark, send, near_next]
        halves.append((start, size, keep, send))

    all_m = own_m + side_m + far_m + farside_m
    mlp_total, mark = weight_grad(places, parts, all_m, high=1, hold=[mark])
    incoming = []
    for index, (start, size, keep, send) in enumerate(halves):
        if index == len(halves) - 1:
            keep, send = after((keep, send), mark)
        far_half = keep.astype(jnp.float32) + send.astype(jnp.float32)
        near_piece = near_keep[start : start + size].astype(jnp.float32)
        near_piece += near_next[start : start + size].astype(jnp.float32)
        own = jnp.where(takes_near, near_piece, far_half)
        other = jnp.where(takes_near, far_half, near_piece).astype(jnp.bfloat16)
        incoming.append((own, lax.ppermute(other, "col", SKIP)))
    mlp_total, mark = weight_grad(places, parts, all_m, low=1, held=mlp_total, hold=[mark, other])

    incoming = jnp.concatenate(
        [own + after(arrived, mark).astype(jnp.float32) for own, arrived in incoming], axis=0
    ) * scale_omega
    terms = row_sum(
        jnp.stack([jnp.sum(incoming, axis=1), jnp.sum(incoming * xhat, axis=1)])
    ) / MODEL_WIDTH
    latent_input_gradient = rstd * (
        incoming - terms[0][:, None] - xhat * terms[1][:, None]
    )
    return latent_input_gradient.astype(jnp.bfloat16), qkv_total, mlp_total


def on_device(
    latents,
    modulation,
    sample_of,
    timestep,
    reward,
    qkv_cotangent,
    mlp_cotangent,
    mlp_preact,
    w_qkv,
    w_mlp,
):
    row_id = lax.axis_index("row")
    col_id = lax.axis_index("col")
    tok_col = latents.shape[0]
    tok_row = qkv_cotangent.shape[0]
    width_row = latents.shape[1]
    samples = reward.shape[0]
    sample_ids = jnp.arange(samples, dtype=jnp.int32)
    onehot = (sample_ids[:, None] == sample_of[None, :]).astype(jnp.float32)
    omega_sample = sample_weights(onehot, timestep, reward)
    omega_tokens = lookup(onehot, omega_sample[:, None])[:, 0]
    omega_rows = lax.dynamic_slice_in_dim(omega_tokens, row_id * tok_row, tok_row)[:, None]
    grad_q = (qkv_cotangent.astype(jnp.float32) * omega_rows).astype(jnp.bfloat16)
    grad_m = (
        mlp_cotangent.astype(jnp.float32) * gelu_slope(mlp_preact.astype(jnp.float32)) * omega_rows
    ).astype(jnp.bfloat16)
    mod_flat = modulation.reshape(samples, 2 * width_row)
    input_float_copy = latents.astype(jnp.float32)
    own_onehot = lax.dynamic_slice_in_dim(onehot, col_id * tok_col, tok_col, 1)
    own_mod = lookup(own_onehot, mod_flat)
    sample_offset = own_mod[:, :width_row]
    sample_scale_factor = 1.0 + own_mod[:, width_row:]
    total_sum, total_square = lax.psum(
        (jnp.sum(input_float_copy, axis=1), jnp.sum(input_float_copy * input_float_copy, axis=1)),
        "row",
    )
    feature_average = (total_sum / MODEL_WIDTH)[:, None]
    inverse_deviation = lax.rsqrt(
        (total_square / MODEL_WIDTH)[:, None] - feature_average * feature_average + EPS
    )
    centered_normalized = (input_float_copy - feature_average) * inverse_deviation
    norm_output = (centered_normalized * sample_scale_factor + sample_offset).astype(jnp.bfloat16)
    normed_all = lax.all_gather(norm_output, "col", axis=0, tiled=True)
    all_q, all_m = (
        lax.all_gather(grad_q, "row", axis=0, tiled=True),
        lax.all_gather(grad_m, "row", axis=0, tiled=True),
    )
    qkv_total = over_tokens(normed_all, all_q)
    mlp_total = over_tokens(normed_all, all_m)
    normed_grad = lax.psum_scatter(
        (against_weight(all_q, w_qkv) + against_weight(all_m, w_mlp)).astype(jnp.bfloat16),
        "col",
        scatter_dimension=0,
        tiled=True,
    ).astype(jnp.float32)
    incoming_gradient = normed_grad * sample_scale_factor
    first_moment_term, second_moment_term = lax.psum(
        (
            jnp.sum(incoming_gradient, axis=1),
            jnp.sum(incoming_gradient * centered_normalized, axis=1),
        ),
        "row",
    )
    latent_input_gradient = inverse_deviation * (
        incoming_gradient
        - (first_moment_term / MODEL_WIDTH)[:, None]
        - centered_normalized * (second_moment_term / MODEL_WIDTH)[:, None]
    )
    return (
        latent_input_gradient.astype(jnp.bfloat16),
        qkv_total.astype(jnp.bfloat16),
        mlp_total.astype(jnp.bfloat16),
    )


def solution(mesh):
    in_specs = (
        P(("groups", "col"), "row"),
        P("groups", None, "row"),
        P("groups"),
        P("groups"),
        P("groups"),
        P(("groups", "row"), "col"),
        P(("groups", "row"), "col"),
        P(("groups", "row"), "col"),
        P("row", "col"),
        P("row", "col"),
    )
    out_specs = (
        P(("groups", "col"), "row"),
        P(("groups", "row"), "col"),
        P(("groups", "row"), "col"),
    )
    small = mesh.shape["row"] == 4 and mesh.shape["col"] == 4
    return jax.shard_map(
        on_grid if small else on_device,
        mesh=mesh,
        in_specs=in_specs,
        out_specs=out_specs,
        check_vma=False,
    )
```

```python
import functools
import math

import jax
import jax.numpy as jnp
from jax import lax
from jax.experimental import pallas as pl
from jax.experimental.pallas import tpu as pltpu
from jax.sharding import PartitionSpec as P

MODEL_WIDTH = 3072
TSTEPS = 1000


EPS = 1e-06
ROOT = math.sqrt(2.0 / math.pi)
CUBE = 0.044715
VMEM_BYTES = 36 * 2**20
QUICK = pl.CostEstimate(flops=1, bytes_accessed=1, transcendentals=0)
MARK = jax.ShapeDtypeStruct((8, 128), jnp.float32)
AHEAD = 2

CORE = [(0, 1), (1, 0), (2, 3), (3, 2)]
CHIP = [(0, 2), (2, 0), (1, 3), (3, 1)]
NEXT, SKIP = CORE, CHIP
PIECES = (160, 96)
STARTS = tuple(sum(PIECES[:k]) for k in range(len(PIECES)))
TURNS = ((0,), (1,))
SWAPS = (((0, 112), (112, 160)), ((0, 96),))
PART = 128


def gelu_slope(value):
    inner = ROOT * (value + CUBE * value * value * value)
    tangent = jnp.tanh(inner)
    return 0.5 * (1.0 + tangent) + 0.5 * value * (1.0 - tangent * tangent) * ROOT * (
        1.0 + 3.0 * CUBE * value * value
    )


def over_tokens(left, right):
    return lax.dot_general(
        left, right, (((0,), (0,)), ((), ())), preferred_element_type=jnp.float32
    )


def against_weight(left, right):
    return lax.dot_general(
        left, right, (((1,), (1,)), ((), ())), preferred_element_type=jnp.float32
    )


def lookup(onehot, table):
    return lax.dot_general(
        onehot,
        table,
        (((0,), (0,)), ((), ())),
        precision=lax.Precision.HIGHEST,
        preferred_element_type=jnp.float32,
    )


def sample_weights(onehot, timestep, reward):
    counts = jnp.sum(onehot, axis=1)
    level = (timestep.astype(jnp.float32) + 0.5) / TSTEPS
    return reward * (0.5 + 1.5 * level * (2.0 - level)) * lax.rsqrt(counts)


def params(**more):
    return pltpu.CompilerParams(vmem_limit_bytes=VMEM_BYTES, **more)


def back_kernel(layout, tile, ordered, seeds, holds, *refs):
    refs = list(refs)
    order = refs.pop(0) if ordered else None
    lefts = [[(place, refs.pop(0)) for place in places] for places in layout]
    weights = [refs.pop(0) for _ in layout]
    seed = refs.pop(0) if seeds else None
    del refs[:holds]
    left_sem, weight_sem, seed_sem = refs[-3:]
    left_buf, weight_buf, total = refs[-6:-3]
    mark, outs = refs[-7], refs[:-7]
    mark[...] = jnp.zeros_like(mark)

    first, place = [], 0
    for index, (start, size) in enumerate(seeds):
        first.append(
            pltpu.make_async_copy(
                seed.at[pl.ds(start, size)], total.at[pl.ds(place, size)], seed_sem.at[index]
            )
        )
        place += size
    for copy in first:
        copy.start()
    tiles, column, number = [], 0, 0
    for group, weight in zip(lefts, weights):
        for low in range(0, weight.shape[1], tile):
            span = pl.ds(column, tile)
            copies = [
                pltpu.make_async_copy(
                    weight.at[:, pl.ds(low, tile)], weight_buf.at[:, span], weight_sem.at[column // tile]
                )
            ]
            for place, left in group:
                copies.append(
                    pltpu.make_async_copy(
                        left.at[:, pl.ds(low, tile)],
                        left_buf.at[pl.ds(place, left.shape[0]), span],
                        left_sem.at[number],
                    )
                )
                number += 1
            tiles.append((span, copies))
            column += tile
    start_tiles = lambda low, high: [copy.start() for _, copies in tiles[low:high] for copy in copies]
    start_tiles(0, AHEAD)
    for copy in first:
        copy.wait()
    for index, (span, copies) in enumerate(tiles):
        start_tiles(index + AHEAD, index + AHEAD + 1)
        for copy in copies:
            copy.wait()
        product = against_weight(left_buf[:, span], weight_buf[:, span])
        if index or seeds:
            total[...] += product
        else:
            total[...] = product
    place = 0
    for index, out in enumerate(outs):
        size = out.shape[0]
        if ordered:
            place = pl.multiple_of(order[index] * size, size)
        out[...] = total[pl.ds(place, size), :].astype(out.dtype)
        place += size


def back(groups, weights, sizes, dtype, tile=768, order=None, seed=None, seeds=(), hold=(), pin=True):
    width = weights[0].shape[0]
    rows = sum(sizes)
    depth = sum(weight.shape[1] for weight in weights)
    layout = [[place for place, _ in group] for group in groups]
    copies = sum(len(group) * (weight.shape[1] // tile) for group, weight in zip(groups, weights))
    operands = [left for group in groups for _, left in group]
    if pin:
        operands = [pltpu.with_memory_space_constraint(left, pltpu.HBM) for left in operands]
    operands += [pltpu.with_memory_space_constraint(weight, pltpu.HBM) for weight in weights]
    if seed is not None:
        operands.append(pltpu.with_memory_space_constraint(seed, pltpu.HBM))
    operands += list(hold)
    in_specs = [pl.BlockSpec(memory_space=pl.ANY)] * len(operands)
    if order is not None:
        operands.insert(0, order)
        in_specs.insert(0, pl.BlockSpec(memory_space=pltpu.SMEM))
    return pl.pallas_call(
        functools.partial(
            back_kernel, layout, tile, order is not None, seeds, len(hold)
        ),
        in_specs=in_specs,
        out_specs=[pl.BlockSpec(memory_space=pltpu.VMEM)] * (len(sizes) + 1),
        out_shape=[
            pltpu.HBM((size, width), dtype) if order is None else jax.ShapeDtypeStruct((size, width), dtype)
            for size in sizes
        ]
        + [MARK],
        scratch_shapes=[
            pltpu.VMEM((rows, depth), jnp.bfloat16),
            pltpu.VMEM((width, depth), jnp.bfloat16),
            pltpu.VMEM((rows, width), jnp.float32),
            pltpu.SemaphoreType.DMA((copies,)),
            pltpu.SemaphoreType.DMA((depth // tile,)),
            pltpu.SemaphoreType.DMA((max(1, len(seeds)),)),
        ],
        compiler_params=params(),
        cost_estimate=QUICK,
    )(*operands)


def weight_kernel(count, holds, places, *refs):
    parts, grads, (out, mark, normed) = refs[:4], refs[4 : 4 + count], refs[-3:]

    @pl.when(pl.program_id(0) == 0)
    def _():
        for index, part in enumerate(parts):
            size = part.shape[0]
            normed[pl.ds(pl.multiple_of(places[index] * size, size), size), :] = part[...]
        mark[...] = jnp.zeros_like(mark)

    joined = jnp.concatenate([grad[...] for grad in grads], axis=0)
    out[...] = over_tokens(normed[...], joined).astype(out.dtype)


def weight_grad(
    places, parts, grads, tile=768, low=0, high=None, held=None, hold=(), pin=True
):
    width = parts[0].shape[1]
    tokens = parts[0].shape[0]
    columns = grads[0].shape[1]
    high = columns // tile if high is None else high
    extra = list(hold) + ([] if held is None else [held])
    arrays = list(parts) + list(grads)
    if pin:
        arrays = [pltpu.with_memory_space_constraint(array, pltpu.HBM) for array in arrays]
    operands = [places] + arrays + extra
    return pl.pallas_call(
        functools.partial(weight_kernel, len(grads), len(extra)),
        grid=(high - low,),
        in_specs=[pl.BlockSpec(memory_space=pltpu.SMEM)]
        + [pl.BlockSpec((tokens // 4, width), lambda i, j=j: (j, 0)) for j in range(4)]
        + [pl.BlockSpec((grad.shape[0], tile), lambda i: (0, i + low)) for grad in grads]
        + [pl.BlockSpec(memory_space=pl.ANY)] * len(extra),
        out_specs=[
            pl.BlockSpec((width, tile), lambda i: (0, i + low)),
            pl.BlockSpec(MARK.shape, lambda i: (0, 0)),
        ],
        out_shape=[jax.ShapeDtypeStruct((width, columns), jnp.bfloat16), MARK],
        scratch_shapes=[pltpu.VMEM((tokens, width), jnp.bfloat16)],
        input_output_aliases={} if held is None else {len(operands) - 1: 0},
        compiler_params=params(),
        cost_estimate=QUICK,
    )(*operands)


def after(value, *others):
    return lax.optimization_barrier((value, others))[0]


def row_sum(pair):
    pair += lax.ppermute(pair, "row", CHIP)
    return pair + lax.ppermute(pair, "row", CORE)


def on_grid(
    latents,
    modulation,
    sample_of,
    timestep,
    reward,
    qkv_cotangent,
    mlp_cotangent,
    mlp_preact,
    w_qkv,
    w_mlp,
):
    row_id = lax.axis_index("row")
    col_id = lax.axis_index("col")
    tok_col, width_row = latents.shape
    tok_row = qkv_cotangent.shape[0]
    samples = reward.shape[0]
    own_first = (row_id ^ col_id) % 2
    order = jnp.stack([own_first, 1 - own_first])

    latents32 = latents.astype(jnp.float32)
    moments = jnp.stack([jnp.sum(latents32, axis=1), jnp.sum(latents32 * latents32, axis=1)])
    far_q = lax.ppermute(after(qkv_cotangent, moments), "row", CHIP)
    moments = row_sum(moments)
    side_q = lax.ppermute(qkv_cotangent, "row", CORE)

    sample_ids = jnp.arange(samples, dtype=jnp.int32)[:, None]
    omega_sample = sample_weights(
        (sample_ids == sample_of[None, :]).astype(jnp.float32), timestep, reward
    )
    own_samples = lax.dynamic_slice_in_dim(sample_of, col_id * tok_col, tok_col)
    own_onehot = (sample_ids == own_samples[None, :]).astype(jnp.float32)
    own_mod = lookup(own_onehot, modulation.reshape(samples, 2 * width_row))
    own_omega = lookup(own_onehot, omega_sample[:, None])
    offset = own_mod[:, :width_row]
    scale = 1.0 + own_mod[:, width_row:]
    mean = (moments[0] / MODEL_WIDTH)[:, None]
    rstd = lax.rsqrt((moments[1] / MODEL_WIDTH)[:, None] - mean * mean + EPS)
    xhat = (latents32 - mean) * rstd
    normed = ((xhat * scale + offset) * own_omega).astype(jnp.bfloat16)
    scale_omega = scale * own_omega
    gathered = lax.all_to_all(
        jnp.broadcast_to(normed[None], (4,) + normed.shape), "col", 0, 0, tiled=False
    )
    parts = [gathered.reshape(-1, width_row)] * 4

    mlp_preact = after(mlp_preact, normed)
    own_m = [
        (
            mlp_cotangent[start : start + size].astype(jnp.float32)
            * gelu_slope(mlp_preact[start : start + size].astype(jnp.float32))
        ).astype(jnp.bfloat16)
        for start, size in zip(STARTS, PIECES)
    ]
    side_m = [lax.ppermute(part, "row", CORE) for part in own_m]
    far_m = [lax.ppermute(part, "row", CHIP) for part in own_m]

    near_keep, near_send, mark = back(
        [
            [(0, qkv_cotangent), (tok_row, side_q)],
            [(start, part) for start, part in zip(STARTS, own_m)]
            + [(tok_row + start, part) for start, part in zip(STARTS, side_m)],
        ],
        [w_qkv, w_mlp],
        [tok_row, tok_row],
        jnp.bfloat16,
        order=order,
    )
    near_next = lax.ppermute(near_send, "col", NEXT)

    ready_q = after(far_q, near_send)
    farside_q = [
        lax.ppermute(ready_q[low : low + PART], "row", CORE) for low in range(0, tok_row, PART)
    ]
    places = jnp.stack([row_id ^ j for j in range(4)])
    takes_near = row_id // 2 == col_id // 2

    far, mark = back(
        [
            [(0, far_q)]
            + [(tok_row + place * PART, part) for place, part in enumerate(farside_q)]
        ],
        [w_qkv],
        [2 * tok_row],
        jnp.float32,
    )
    q_parts = [qkv_cotangent, side_q, far_q] + farside_q
    ready, farside_m, halves = [mark], [], []
    for index, turn in enumerate(TURNS):
        for k in turn:
            farside_m.append(lax.ppermute(after(far_m[k], *ready), "row", CORE))
        start, size = STARTS[turn[0]], sum(PIECES[k] for k in turn)
        keep, send, mark = back(
            [
                [(STARTS[k] - start, far_m[k]) for k in turn]
                + [(size + STARTS[k] - start, farside_m[k]) for k in turn]
            ],
            [w_mlp],
            [size, size],
            jnp.bfloat16,
            order=order,
            seed=far,
            seeds=((start, size), (tok_row + start, size)),
            hold=[mark],
            pin=False,
        )
        send = lax.ppermute(send, "col", NEXT)
        if index == 0:
            qkv_total, mark = weight_grad(places, parts, q_parts, hold=[mark])
            ready = [mark, send, near_next]
        halves.append((start, size, keep, send))

    all_m = own_m + side_m + far_m + farside_m
    mlp_total, mark = weight_grad(places, parts, all_m, high=1, hold=[mark])
    incoming = []
    for turn, (start, size, keep, send) in enumerate(halves):
        if turn == len(halves) - 1:
            keep, send = after((keep, send), mark, *[arrived for _, arrived in incoming])
        far_half = keep.astype(jnp.float32) + send.astype(jnp.float32)
        near_piece = near_keep[start : start + size].astype(jnp.float32)
        near_piece += near_next[start : start + size].astype(jnp.float32)
        own = jnp.where(takes_near, near_piece, far_half)
        other = jnp.where(takes_near, far_half, near_piece).astype(jnp.bfloat16)
        for low, high in SWAPS[turn]:
            incoming.append((own[low:high], lax.ppermute(other[low:high], "col", SKIP)))
    mlp_total, mark = weight_grad(places, parts, all_m, low=1, held=mlp_total, hold=[mark, other])

    incoming = jnp.concatenate(
        [own + after(arrived, mark).astype(jnp.float32) for own, arrived in incoming], axis=0
    ) * scale_omega
    terms = row_sum(
        jnp.stack([jnp.sum(incoming, axis=1), jnp.sum(incoming * xhat, axis=1)])
    ) / MODEL_WIDTH
    latent_input_gradient = rstd * (
        incoming - terms[0][:, None] - xhat * terms[1][:, None]
    )
    return latent_input_gradient.astype(jnp.bfloat16), qkv_total, mlp_total


def on_device(
    latents,
    modulation,
    sample_of,
    timestep,
    reward,
    qkv_cotangent,
    mlp_cotangent,
    mlp_preact,
    w_qkv,
    w_mlp,
):
    row_id = lax.axis_index("row")
    col_id = lax.axis_index("col")
    tok_col = latents.shape[0]
    tok_row = qkv_cotangent.shape[0]
    width_row = latents.shape[1]
    samples = reward.shape[0]
    sample_ids = jnp.arange(samples, dtype=jnp.int32)
    onehot = (sample_ids[:, None] == sample_of[None, :]).astype(jnp.float32)
    omega_sample = sample_weights(onehot, timestep, reward)
    omega_tokens = lookup(onehot, omega_sample[:, None])[:, 0]
    omega_rows = lax.dynamic_slice_in_dim(omega_tokens, row_id * tok_row, tok_row)[:, None]
    grad_q = (qkv_cotangent.astype(jnp.float32) * omega_rows).astype(jnp.bfloat16)
    grad_m = (
        mlp_cotangent.astype(jnp.float32) * gelu_slope(mlp_preact.astype(jnp.float32)) * omega_rows
    ).astype(jnp.bfloat16)
    mod_flat = modulation.reshape(samples, 2 * width_row)
    input_float_copy = latents.astype(jnp.float32)
    own_onehot = lax.dynamic_slice_in_dim(onehot, col_id * tok_col, tok_col, 1)
    own_mod = lookup(own_onehot, mod_flat)
    sample_offset = own_mod[:, :width_row]
    sample_scale_factor = 1.0 + own_mod[:, width_row:]
    total_sum, total_square = lax.psum(
        (jnp.sum(input_float_copy, axis=1), jnp.sum(input_float_copy * input_float_copy, axis=1)),
        "row",
    )
    feature_average = (total_sum / MODEL_WIDTH)[:, None]
    inverse_deviation = lax.rsqrt(
        (total_square / MODEL_WIDTH)[:, None] - feature_average * feature_average + EPS
    )
    centered_normalized = (input_float_copy - feature_average) * inverse_deviation
    norm_output = (centered_normalized * sample_scale_factor + sample_offset).astype(jnp.bfloat16)
    normed_all = lax.all_gather(norm_output, "col", axis=0, tiled=True)
    all_q, all_m = (
        lax.all_gather(grad_q, "row", axis=0, tiled=True),
        lax.all_gather(grad_m, "row", axis=0, tiled=True),
    )
    qkv_total = over_tokens(normed_all, all_q)
    mlp_total = over_tokens(normed_all, all_m)
    normed_grad = lax.psum_scatter(
        (against_weight(all_q, w_qkv) + against_weight(all_m, w_mlp)).astype(jnp.bfloat16),
        "col",
        scatter_dimension=0,
        tiled=True,
    ).astype(jnp.float32)
    incoming_gradient = normed_grad * sample_scale_factor
    first_moment_term, second_moment_term = lax.psum(
        (
            jnp.sum(incoming_gradient, axis=1),
            jnp.sum(incoming_gradient * centered_normalized, axis=1),
        ),
        "row",
    )
    latent_input_gradient = inverse_deviation * (
        incoming_gradient
        - (first_moment_term / MODEL_WIDTH)[:, None]
        - centered_normalized * (second_moment_term / MODEL_WIDTH)[:, None]
    )
    return (
        latent_input_gradient.astype(jnp.bfloat16),
        qkv_total.astype(jnp.bfloat16),
        mlp_total.astype(jnp.bfloat16),
    )


def solution(mesh):
    in_specs = (
        P(("groups", "col"), "row"),
        P("groups", None, "row"),
        P("groups"),
        P("groups"),
        P("groups"),
        P(("groups", "row"), "col"),
        P(("groups", "row"), "col"),
        P(("groups", "row"), "col"),
        P("row", "col"),
        P("row", "col"),
    )
    out_specs = (
        P(("groups", "col"), "row"),
        P(("groups", "row"), "col"),
        P(("groups", "row"), "col"),
    )
    small = mesh.shape["row"] == 4 and mesh.shape["col"] == 4
    return jax.shard_map(
        on_grid if small else on_device,
        mesh=mesh,
        in_specs=in_specs,
        out_specs=out_specs,
        check_vma=False,
    )
```

```python
import functools
import math

import jax
import jax.numpy as jnp
from jax import lax
from jax.experimental import pallas as pl
from jax.experimental.pallas import tpu as pltpu
from jax.sharding import PartitionSpec as P

MODEL_WIDTH = 3072
TSTEPS = 1000


EPS = 1e-06
ROOT = math.sqrt(2.0 / math.pi)
CUBE = 0.044715
VMEM_BYTES = 36 * 2**20
QUICK = pl.CostEstimate(flops=1, bytes_accessed=1, transcendentals=0)
MARK = jax.ShapeDtypeStruct((8, 128), jnp.float32)
AHEAD = 2

CORE = [(0, 1), (1, 0), (2, 3), (3, 2)]
CHIP = [(0, 2), (2, 0), (1, 3), (3, 1)]
BOTH = [(0, 3), (3, 0), (1, 2), (2, 1)]
NEXT, SKIP = CORE, CHIP
PIECES = (160, 96)
STARTS = tuple(sum(PIECES[:k]) for k in range(len(PIECES)))
TURNS = ((0,), (1,))
SWAPS = (((0, 112), (112, 160)), ((0, 96),))
PART = 128


def gelu_slope(value):
    inner = ROOT * (value + CUBE * value * value * value)
    tangent = jnp.tanh(inner)
    return 0.5 * (1.0 + tangent) + 0.5 * value * (1.0 - tangent * tangent) * ROOT * (
        1.0 + 3.0 * CUBE * value * value
    )


def over_tokens(left, right):
    return lax.dot_general(
        left, right, (((0,), (0,)), ((), ())), preferred_element_type=jnp.float32
    )


def against_weight(left, right):
    return lax.dot_general(
        left, right, (((1,), (1,)), ((), ())), preferred_element_type=jnp.float32
    )


def lookup(onehot, table):
    return lax.dot_general(
        onehot,
        table,
        (((0,), (0,)), ((), ())),
        precision=lax.Precision.HIGHEST,
        preferred_element_type=jnp.float32,
    )


def sample_weights(onehot, timestep, reward):
    counts = jnp.sum(onehot, axis=1)
    level = (timestep.astype(jnp.float32) + 0.5) / TSTEPS
    return reward * (0.5 + 1.5 * level * (2.0 - level)) * lax.rsqrt(counts)


def params(**more):
    return pltpu.CompilerParams(vmem_limit_bytes=VMEM_BYTES, **more)


def back_kernel(layout, tile, ordered, seeds, holds, *refs):
    refs = list(refs)
    order = refs.pop(0) if ordered else None
    lefts = [[(place, refs.pop(0)) for place in places] for places in layout]
    weights = [refs.pop(0) for _ in layout]
    seed = refs.pop(0) if seeds else None
    del refs[:holds]
    left_sem, weight_sem, seed_sem = refs[-3:]
    left_buf, weight_buf, total = refs[-6:-3]
    mark, outs = refs[-7], refs[:-7]
    mark[...] = jnp.zeros_like(mark)

    first, place = [], 0
    for index, (start, size) in enumerate(seeds):
        first.append(
            pltpu.make_async_copy(
                seed.at[pl.ds(start, size)], total.at[pl.ds(place, size)], seed_sem.at[index]
            )
        )
        place += size
    for copy in first:
        copy.start()
    tiles, column, number = [], 0, 0
    for group, weight in zip(lefts, weights):
        for low in range(0, weight.shape[1], tile):
            span = pl.ds(column, tile)
            copies = [
                pltpu.make_async_copy(
                    weight.at[:, pl.ds(low, tile)], weight_buf.at[:, span], weight_sem.at[column // tile]
                )
            ]
            for place, left in group:
                copies.append(
                    pltpu.make_async_copy(
                        left.at[:, pl.ds(low, tile)],
                        left_buf.at[pl.ds(place, left.shape[0]), span],
                        left_sem.at[number],
                    )
                )
                number += 1
            tiles.append((span, copies))
            column += tile
    start_tiles = lambda low, high: [copy.start() for _, copies in tiles[low:high] for copy in copies]
    start_tiles(0, AHEAD)
    for copy in first:
        copy.wait()
    for index, (span, copies) in enumerate(tiles):
        start_tiles(index + AHEAD, index + AHEAD + 1)
        for copy in copies:
            copy.wait()
        product = against_weight(left_buf[:, span], weight_buf[:, span])
        if index or seeds:
            total[...] += product
        else:
            total[...] = product
    place = 0
    for index, out in enumerate(outs):
        size = out.shape[0]
        if ordered:
            place = pl.multiple_of(order[index] * size, size)
        out[...] = total[pl.ds(place, size), :].astype(out.dtype)
        place += size


def back(groups, weights, sizes, dtype, tile=768, order=None, seed=None, seeds=(), hold=(), pin=True):
    width = weights[0].shape[0]
    rows = sum(sizes)
    depth = sum(weight.shape[1] for weight in weights)
    layout = [[place for place, _ in group] for group in groups]
    copies = sum(len(group) * (weight.shape[1] // tile) for group, weight in zip(groups, weights))
    operands = [left for group in groups for _, left in group]
    if pin:
        operands = [pltpu.with_memory_space_constraint(left, pltpu.HBM) for left in operands]
    operands += [pltpu.with_memory_space_constraint(weight, pltpu.HBM) for weight in weights]
    if seed is not None:
        operands.append(pltpu.with_memory_space_constraint(seed, pltpu.HBM))
    operands += list(hold)
    in_specs = [pl.BlockSpec(memory_space=pl.ANY)] * len(operands)
    if order is not None:
        operands.insert(0, order)
        in_specs.insert(0, pl.BlockSpec(memory_space=pltpu.SMEM))
    return pl.pallas_call(
        functools.partial(
            back_kernel, layout, tile, order is not None, seeds, len(hold)
        ),
        in_specs=in_specs,
        out_specs=[pl.BlockSpec(memory_space=pltpu.VMEM)] * (len(sizes) + 1),
        out_shape=[
            pltpu.HBM((size, width), dtype) if order is None else jax.ShapeDtypeStruct((size, width), dtype)
            for size in sizes
        ]
        + [MARK],
        scratch_shapes=[
            pltpu.VMEM((rows, depth), jnp.bfloat16),
            pltpu.VMEM((width, depth), jnp.bfloat16),
            pltpu.VMEM((rows, width), jnp.float32),
            pltpu.SemaphoreType.DMA((copies,)),
            pltpu.SemaphoreType.DMA((depth // tile,)),
            pltpu.SemaphoreType.DMA((max(1, len(seeds)),)),
        ],
        compiler_params=params(),
        cost_estimate=QUICK,
    )(*operands)


def weight_kernel(count, holds, places, *refs):
    parts, grads, (out, mark, normed) = refs[:4], refs[4 : 4 + count], refs[-3:]

    @pl.when(pl.program_id(0) == 0)
    def _():
        for index, part in enumerate(parts):
            size = part.shape[0]
            normed[pl.ds(pl.multiple_of(places[index] * size, size), size), :] = part[...]
        mark[...] = jnp.zeros_like(mark)

    joined = jnp.concatenate([grad[...] for grad in grads], axis=0)
    out[...] = over_tokens(normed[...], joined).astype(out.dtype)


def weight_grad(
    places, parts, grads, tile=768, low=0, high=None, held=None, hold=(), pin=True
):
    width = parts[0].shape[1]
    tokens = parts[0].shape[0]
    columns = grads[0].shape[1]
    high = columns // tile if high is None else high
    extra = list(hold) + ([] if held is None else [held])
    arrays = list(parts) + list(grads)
    if pin:
        arrays = [pltpu.with_memory_space_constraint(array, pltpu.HBM) for array in arrays]
    operands = [places] + arrays + extra
    return pl.pallas_call(
        functools.partial(weight_kernel, len(grads), len(extra)),
        grid=(high - low,),
        in_specs=[pl.BlockSpec(memory_space=pltpu.SMEM)]
        + [pl.BlockSpec((tokens // 4, width), lambda i, j=j: (j, 0)) for j in range(4)]
        + [pl.BlockSpec((grad.shape[0], tile), lambda i: (0, i + low)) for grad in grads]
        + [pl.BlockSpec(memory_space=pl.ANY)] * len(extra),
        out_specs=[
            pl.BlockSpec((width, tile), lambda i: (0, i + low)),
            pl.BlockSpec(MARK.shape, lambda i: (0, 0)),
        ],
        out_shape=[jax.ShapeDtypeStruct((width, columns), jnp.bfloat16), MARK],
        scratch_shapes=[pltpu.VMEM((tokens, width), jnp.bfloat16)],
        input_output_aliases={} if held is None else {len(operands) - 1: 0},
        compiler_params=params(),
        cost_estimate=QUICK,
    )(*operands)


def after(value, *others):
    return lax.optimization_barrier((value, others))[0]


def row_sum(pair):
    pair += lax.ppermute(pair, "row", CHIP)
    return pair + lax.ppermute(pair, "row", CORE)


def row_sum_direct(pair):
    return (
        pair
        + lax.ppermute(pair, "row", CORE)
        + lax.ppermute(pair, "row", CHIP)
        + lax.ppermute(pair, "row", BOTH)
    )


def on_grid(
    latents,
    modulation,
    sample_of,
    timestep,
    reward,
    qkv_cotangent,
    mlp_cotangent,
    mlp_preact,
    w_qkv,
    w_mlp,
):
    row_id = lax.axis_index("row")
    col_id = lax.axis_index("col")
    tok_col, width_row = latents.shape
    tok_row = qkv_cotangent.shape[0]
    samples = reward.shape[0]
    own_first = (row_id ^ col_id) % 2
    order = jnp.stack([own_first, 1 - own_first])

    latents32 = latents.astype(jnp.float32)
    moments = jnp.stack([jnp.sum(latents32, axis=1), jnp.sum(latents32 * latents32, axis=1)])
    far_q = lax.ppermute(after(qkv_cotangent, moments), "row", CHIP)
    moments = row_sum(moments)
    side_q = lax.ppermute(qkv_cotangent, "row", CORE)

    sample_ids = jnp.arange(samples, dtype=jnp.int32)[:, None]
    omega_sample = sample_weights(
        (sample_ids == sample_of[None, :]).astype(jnp.float32), timestep, reward
    )
    own_samples = lax.dynamic_slice_in_dim(sample_of, col_id * tok_col, tok_col)
    own_onehot = (sample_ids == own_samples[None, :]).astype(jnp.float32)
    own_mod = lookup(own_onehot, modulation.reshape(samples, 2 * width_row))
    own_omega = lookup(own_onehot, omega_sample[:, None])
    offset = own_mod[:, :width_row]
    scale = 1.0 + own_mod[:, width_row:]
    mean = (moments[0] / MODEL_WIDTH)[:, None]
    rstd = lax.rsqrt((moments[1] / MODEL_WIDTH)[:, None] - mean * mean + EPS)
    xhat = (latents32 - mean) * rstd
    normed = ((xhat * scale + offset) * own_omega).astype(jnp.bfloat16)
    scale_omega = scale * own_omega
    gathered = lax.all_to_all(
        jnp.broadcast_to(normed[None], (4,) + normed.shape), "col", 0, 0, tiled=False
    )
    parts = [gathered.reshape(-1, width_row)] * 4

    mlp_preact = after(mlp_preact, normed)
    own_m = [
        (
            mlp_cotangent[start : start + size].astype(jnp.float32)
            * gelu_slope(mlp_preact[start : start + size].astype(jnp.float32))
        ).astype(jnp.bfloat16)
        for start, size in zip(STARTS, PIECES)
    ]
    side_m = [lax.ppermute(part, "row", CORE) for part in own_m]
    far_m = [lax.ppermute(part, "row", CHIP) for part in own_m]

    near_keep, near_send, mark = back(
        [
            [(0, qkv_cotangent), (tok_row, side_q)],
            [(start, part) for start, part in zip(STARTS, own_m)]
            + [(tok_row + start, part) for start, part in zip(STARTS, side_m)],
        ],
        [w_qkv, w_mlp],
        [tok_row, tok_row],
        jnp.bfloat16,
        order=order,
    )
    near_next = lax.ppermute(near_send, "col", NEXT)

    ready_q = after(far_q, near_send)
    farside_q = [
        lax.ppermute(ready_q[low : low + PART], "row", CORE) for low in range(0, tok_row, PART)
    ]
    places = jnp.stack([row_id ^ j for j in range(4)])
    takes_near = row_id // 2 == col_id // 2

    far, mark = back(
        [
            [(0, far_q)]
            + [(tok_row + place * PART, part) for place, part in enumerate(farside_q)]
        ],
        [w_qkv],
        [2 * tok_row],
        jnp.float32,
    )
    q_parts = [qkv_cotangent, side_q, far_q] + farside_q
    ready, farside_m, halves = [mark], [], []
    for index, turn in enumerate(TURNS):
        for k in turn:
            farside_m.append(lax.ppermute(after(far_m[k], *ready), "row", CORE))
        start, size = STARTS[turn[0]], sum(PIECES[k] for k in turn)
        keep, send, mark = back(
            [
                [(STARTS[k] - start, far_m[k]) for k in turn]
                + [(size + STARTS[k] - start, farside_m[k]) for k in turn]
            ],
            [w_mlp],
            [size, size],
            jnp.bfloat16,
            order=order,
            seed=far,
            seeds=((start, size), (tok_row + start, size)),
            hold=[mark],
            pin=False,
        )
        send = lax.ppermute(send, "col", NEXT)
        if index == 0:
            qkv_total, mark = weight_grad(places, parts, q_parts, hold=[mark])
            ready = [mark, send, near_next]
        halves.append((start, size, keep, send))

    all_m = own_m + side_m + far_m + farside_m
    mlp_total, mark = weight_grad(places, parts, all_m, tile=1024, high=1, hold=[mark])
    incoming = []
    for turn, (start, size, keep, send) in enumerate(halves):
        if turn == len(halves) - 1:
            keep, send = after((keep, send), mark, *[arrived for _, arrived in incoming])
        far_half = keep.astype(jnp.float32) + send.astype(jnp.float32)
        near_piece = near_keep[start : start + size].astype(jnp.float32)
        near_piece += near_next[start : start + size].astype(jnp.float32)
        own = jnp.where(takes_near, near_piece, far_half)
        other = jnp.where(takes_near, far_half, near_piece).astype(jnp.bfloat16)
        for low, high in SWAPS[turn]:
            incoming.append((own[low:high], lax.ppermute(other[low:high], "col", SKIP)))
    mlp_total, mark = weight_grad(
        places, parts, all_m, tile=1024, low=1, held=mlp_total, hold=[mark, other]
    )

    incoming = jnp.concatenate(
        [own + after(arrived, mark).astype(jnp.float32) for own, arrived in incoming], axis=0
    ) * scale_omega
    terms = row_sum_direct(
        jnp.stack([jnp.sum(incoming, axis=1), jnp.sum(incoming * xhat, axis=1)])
    ) / MODEL_WIDTH
    latent_input_gradient = rstd * (
        incoming - terms[0][:, None] - xhat * terms[1][:, None]
    )
    return latent_input_gradient.astype(jnp.bfloat16), qkv_total, mlp_total


def on_device(
    latents,
    modulation,
    sample_of,
    timestep,
    reward,
    qkv_cotangent,
    mlp_cotangent,
    mlp_preact,
    w_qkv,
    w_mlp,
):
    row_id = lax.axis_index("row")
    col_id = lax.axis_index("col")
    tok_col = latents.shape[0]
    tok_row = qkv_cotangent.shape[0]
    width_row = latents.shape[1]
    samples = reward.shape[0]
    sample_ids = jnp.arange(samples, dtype=jnp.int32)
    onehot = (sample_ids[:, None] == sample_of[None, :]).astype(jnp.float32)
    omega_sample = sample_weights(onehot, timestep, reward)
    omega_tokens = lookup(onehot, omega_sample[:, None])[:, 0]
    omega_rows = lax.dynamic_slice_in_dim(omega_tokens, row_id * tok_row, tok_row)[:, None]
    grad_q = (qkv_cotangent.astype(jnp.float32) * omega_rows).astype(jnp.bfloat16)
    grad_m = (
        mlp_cotangent.astype(jnp.float32) * gelu_slope(mlp_preact.astype(jnp.float32)) * omega_rows
    ).astype(jnp.bfloat16)
    mod_flat = modulation.reshape(samples, 2 * width_row)
    input_float_copy = latents.astype(jnp.float32)
    own_onehot = lax.dynamic_slice_in_dim(onehot, col_id * tok_col, tok_col, 1)
    own_mod = lookup(own_onehot, mod_flat)
    sample_offset = own_mod[:, :width_row]
    sample_scale_factor = 1.0 + own_mod[:, width_row:]
    total_sum, total_square = lax.psum(
        (jnp.sum(input_float_copy, axis=1), jnp.sum(input_float_copy * input_float_copy, axis=1)),
        "row",
    )
    feature_average = (total_sum / MODEL_WIDTH)[:, None]
    inverse_deviation = lax.rsqrt(
        (total_square / MODEL_WIDTH)[:, None] - feature_average * feature_average + EPS
    )
    centered_normalized = (input_float_copy - feature_average) * inverse_deviation
    norm_output = (centered_normalized * sample_scale_factor + sample_offset).astype(jnp.bfloat16)
    normed_all = lax.all_gather(norm_output, "col", axis=0, tiled=True)
    all_q, all_m = (
        lax.all_gather(grad_q, "row", axis=0, tiled=True),
        lax.all_gather(grad_m, "row", axis=0, tiled=True),
    )
    qkv_total = over_tokens(normed_all, all_q)
    mlp_total = over_tokens(normed_all, all_m)
    normed_grad = lax.psum_scatter(
        (against_weight(all_q, w_qkv) + against_weight(all_m, w_mlp)).astype(jnp.bfloat16),
        "col",
        scatter_dimension=0,
        tiled=True,
    ).astype(jnp.float32)
    incoming_gradient = normed_grad * sample_scale_factor
    first_moment_term, second_moment_term = lax.psum(
        (
            jnp.sum(incoming_gradient, axis=1),
            jnp.sum(incoming_gradient * centered_normalized, axis=1),
        ),
        "row",
    )
    latent_input_gradient = inverse_deviation * (
        incoming_gradient
        - (first_moment_term / MODEL_WIDTH)[:, None]
        - centered_normalized * (second_moment_term / MODEL_WIDTH)[:, None]
    )
    return (
        latent_input_gradient.astype(jnp.bfloat16),
        qkv_total.astype(jnp.bfloat16),
        mlp_total.astype(jnp.bfloat16),
    )


def solution(mesh):
    in_specs = (
        P(("groups", "col"), "row"),
        P("groups", None, "row"),
        P("groups"),
        P("groups"),
        P("groups"),
        P(("groups", "row"), "col"),
        P(("groups", "row"), "col"),
        P(("groups", "row"), "col"),
        P("row", "col"),
        P("row", "col"),
    )
    out_specs = (
        P(("groups", "col"), "row"),
        P(("groups", "row"), "col"),
        P(("groups", "row"), "col"),
    )
    small = mesh.shape["row"] == 4 and mesh.shape["col"] == 4
    return jax.shard_map(
        on_grid if small else on_device,
        mesh=mesh,
        in_specs=in_specs,
        out_specs=out_specs,
        check_vma=False,
    )
```

```python
import functools
import math

import jax
import jax.numpy as jnp
from jax import lax
from jax.experimental import pallas as pl
from jax.experimental.pallas import tpu as pltpu
from jax.sharding import PartitionSpec as P

MODEL_WIDTH = 3072
TSTEPS = 1000


EPS = 1e-06
ROOT = math.sqrt(2.0 / math.pi)
CUBE = 0.044715
VMEM_BYTES = 36 * 2**20
QUICK = pl.CostEstimate(flops=1, bytes_accessed=1, transcendentals=0)
MARK = jax.ShapeDtypeStruct((8, 128), jnp.float32)
AHEAD = 2

CORE = [(0, 1), (1, 0), (2, 3), (3, 2)]
CHIP = [(0, 2), (2, 0), (1, 3), (3, 1)]
BOTH = [(0, 3), (3, 0), (1, 2), (2, 1)]
NEXT, SKIP = CORE, CHIP
PIECES = (144, 112)
STARTS = tuple(sum(PIECES[:k]) for k in range(len(PIECES)))
TURNS = ((0,), (1,))
SWAPS = (((0, 112), (112, 144)), ((0, 112),))
PART = 128


def gelu_slope(value):
    inner = ROOT * (value + CUBE * value * value * value)
    tangent = jnp.tanh(inner)
    return 0.5 * (1.0 + tangent) + 0.5 * value * (1.0 - tangent * tangent) * ROOT * (
        1.0 + 3.0 * CUBE * value * value
    )


def over_tokens(left, right):
    return lax.dot_general(
        left, right, (((0,), (0,)), ((), ())), preferred_element_type=jnp.float32
    )


def against_weight(left, right):
    return lax.dot_general(
        left, right, (((1,), (1,)), ((), ())), preferred_element_type=jnp.float32
    )


def lookup(onehot, table):
    return lax.dot_general(
        onehot,
        table,
        (((0,), (0,)), ((), ())),
        precision=lax.Precision.HIGHEST,
        preferred_element_type=jnp.float32,
    )


def sample_weights(onehot, timestep, reward):
    counts = jnp.sum(onehot, axis=1)
    level = (timestep.astype(jnp.float32) + 0.5) / TSTEPS
    return reward * (0.5 + 1.5 * level * (2.0 - level)) * lax.rsqrt(counts)


def params(**more):
    return pltpu.CompilerParams(vmem_limit_bytes=VMEM_BYTES, **more)


def back_kernel(layout, tile, ordered, seeds, holds, *refs):
    refs = list(refs)
    order = refs.pop(0) if ordered else None
    lefts = [[(place, refs.pop(0)) for place in places] for places in layout]
    weights = [refs.pop(0) for _ in layout]
    seed = refs.pop(0) if seeds else None
    del refs[:holds]
    left_sem, weight_sem, seed_sem = refs[-3:]
    left_buf, weight_buf, total = refs[-6:-3]
    mark, outs = refs[-7], refs[:-7]
    mark[...] = jnp.zeros_like(mark)

    first, place = [], 0
    for index, (start, size) in enumerate(seeds):
        first.append(
            pltpu.make_async_copy(
                seed.at[pl.ds(start, size)], total.at[pl.ds(place, size)], seed_sem.at[index]
            )
        )
        place += size
    for copy in first:
        copy.start()
    tiles, column, number = [], 0, 0
    for group, weight in zip(lefts, weights):
        for low in range(0, weight.shape[1], tile):
            span = pl.ds(column, tile)
            copies = [
                pltpu.make_async_copy(
                    weight.at[:, pl.ds(low, tile)], weight_buf.at[:, span], weight_sem.at[column // tile]
                )
            ]
            for place, left in group:
                copies.append(
                    pltpu.make_async_copy(
                        left.at[:, pl.ds(low, tile)],
                        left_buf.at[pl.ds(place, left.shape[0]), span],
                        left_sem.at[number],
                    )
                )
                number += 1
            tiles.append((span, copies))
            column += tile
    start_tiles = lambda low, high: [copy.start() for _, copies in tiles[low:high] for copy in copies]
    start_tiles(0, AHEAD)
    for copy in first:
        copy.wait()
    for index, (span, copies) in enumerate(tiles):
        start_tiles(index + AHEAD, index + AHEAD + 1)
        for copy in copies:
            copy.wait()
        product = against_weight(left_buf[:, span], weight_buf[:, span])
        if index or seeds:
            total[...] += product
        else:
            total[...] = product
    place = 0
    for index, out in enumerate(outs):
        size = out.shape[0]
        if ordered:
            place = pl.multiple_of(order[index] * size, size)
        out[...] = total[pl.ds(place, size), :].astype(out.dtype)
        place += size


def back(groups, weights, sizes, dtype, tile=768, order=None, seed=None, seeds=(), hold=(), pin=True):
    width = weights[0].shape[0]
    rows = sum(sizes)
    depth = sum(weight.shape[1] for weight in weights)
    layout = [[place for place, _ in group] for group in groups]
    copies = sum(len(group) * (weight.shape[1] // tile) for group, weight in zip(groups, weights))
    operands = [left for group in groups for _, left in group]
    if pin:
        operands = [pltpu.with_memory_space_constraint(left, pltpu.HBM) for left in operands]
    operands += [pltpu.with_memory_space_constraint(weight, pltpu.HBM) for weight in weights]
    if seed is not None:
        operands.append(pltpu.with_memory_space_constraint(seed, pltpu.HBM))
    operands += list(hold)
    in_specs = [pl.BlockSpec(memory_space=pl.ANY)] * len(operands)
    if order is not None:
        operands.insert(0, order)
        in_specs.insert(0, pl.BlockSpec(memory_space=pltpu.SMEM))
    return pl.pallas_call(
        functools.partial(
            back_kernel, layout, tile, order is not None, seeds, len(hold)
        ),
        in_specs=in_specs,
        out_specs=[pl.BlockSpec(memory_space=pltpu.VMEM)] * (len(sizes) + 1),
        out_shape=[
            pltpu.HBM((size, width), dtype) if order is None else jax.ShapeDtypeStruct((size, width), dtype)
            for size in sizes
        ]
        + [MARK],
        scratch_shapes=[
            pltpu.VMEM((rows, depth), jnp.bfloat16),
            pltpu.VMEM((width, depth), jnp.bfloat16),
            pltpu.VMEM((rows, width), jnp.float32),
            pltpu.SemaphoreType.DMA((copies,)),
            pltpu.SemaphoreType.DMA((depth // tile,)),
            pltpu.SemaphoreType.DMA((max(1, len(seeds)),)),
        ],
        compiler_params=params(),
        cost_estimate=QUICK,
    )(*operands)


def weight_kernel(count, holds, places, *refs):
    parts, grads, (out, mark, normed) = refs[:4], refs[4 : 4 + count], refs[-3:]

    @pl.when(pl.program_id(0) == 0)
    def _():
        for index, part in enumerate(parts):
            size = part.shape[0]
            normed[pl.ds(pl.multiple_of(places[index] * size, size), size), :] = part[...]
        mark[...] = jnp.zeros_like(mark)

    joined = jnp.concatenate([grad[...] for grad in grads], axis=0)
    out[...] = over_tokens(normed[...], joined).astype(out.dtype)


def weight_grad(
    places, parts, grads, tile=768, low=0, high=None, held=None, hold=(), pin=True
):
    width = parts[0].shape[1]
    tokens = parts[0].shape[0]
    columns = grads[0].shape[1]
    high = columns // tile if high is None else high
    extra = list(hold) + ([] if held is None else [held])
    arrays = list(parts) + list(grads)
    if pin:
        arrays = [pltpu.with_memory_space_constraint(array, pltpu.HBM) for array in arrays]
    operands = [places] + arrays + extra
    return pl.pallas_call(
        functools.partial(weight_kernel, len(grads), len(extra)),
        grid=(high - low,),
        in_specs=[pl.BlockSpec(memory_space=pltpu.SMEM)]
        + [pl.BlockSpec((tokens // 4, width), lambda i, j=j: (j, 0)) for j in range(4)]
        + [pl.BlockSpec((grad.shape[0], tile), lambda i: (0, i + low)) for grad in grads]
        + [pl.BlockSpec(memory_space=pl.ANY)] * len(extra),
        out_specs=[
            pl.BlockSpec((width, tile), lambda i: (0, i + low)),
            pl.BlockSpec(MARK.shape, lambda i: (0, 0)),
        ],
        out_shape=[jax.ShapeDtypeStruct((width, columns), jnp.bfloat16), MARK],
        scratch_shapes=[pltpu.VMEM((tokens, width), jnp.bfloat16)],
        input_output_aliases={} if held is None else {len(operands) - 1: 0},
        compiler_params=params(),
        cost_estimate=QUICK,
    )(*operands)


def after(value, *others):
    return lax.optimization_barrier((value, others))[0]


def row_sum(pair):
    pair += lax.ppermute(pair, "row", CHIP)
    return pair + lax.ppermute(pair, "row", CORE)


def row_sum_direct(pair):
    return (
        pair
        + lax.ppermute(pair, "row", CORE)
        + lax.ppermute(pair, "row", CHIP)
        + lax.ppermute(pair, "row", BOTH)
    )


def on_grid(
    latents,
    modulation,
    sample_of,
    timestep,
    reward,
    qkv_cotangent,
    mlp_cotangent,
    mlp_preact,
    w_qkv,
    w_mlp,
):
    row_id = lax.axis_index("row")
    col_id = lax.axis_index("col")
    tok_col, width_row = latents.shape
    tok_row = qkv_cotangent.shape[0]
    samples = reward.shape[0]
    own_first = (row_id ^ col_id) % 2
    order = jnp.stack([own_first, 1 - own_first])

    latents32 = latents.astype(jnp.float32)
    moments = jnp.stack([jnp.sum(latents32, axis=1), jnp.sum(latents32 * latents32, axis=1)])
    far_q = lax.ppermute(after(qkv_cotangent, moments), "row", CHIP)
    moments = row_sum(moments)
    side_q = lax.ppermute(qkv_cotangent, "row", CORE)

    sample_ids = jnp.arange(samples, dtype=jnp.int32)[:, None]
    omega_sample = sample_weights(
        (sample_ids == sample_of[None, :]).astype(jnp.float32), timestep, reward
    )
    own_samples = lax.dynamic_slice_in_dim(sample_of, col_id * tok_col, tok_col)
    own_onehot = (sample_ids == own_samples[None, :]).astype(jnp.float32)
    own_mod = lookup(own_onehot, modulation.reshape(samples, 2 * width_row))
    own_omega = lookup(own_onehot, omega_sample[:, None])
    offset = own_mod[:, :width_row]
    scale = 1.0 + own_mod[:, width_row:]
    mean = (moments[0] / MODEL_WIDTH)[:, None]
    rstd = lax.rsqrt((moments[1] / MODEL_WIDTH)[:, None] - mean * mean + EPS)
    xhat = (latents32 - mean) * rstd
    normed = ((xhat * scale + offset) * own_omega).astype(jnp.bfloat16)
    scale_omega = scale * own_omega
    gathered = lax.all_to_all(
        jnp.broadcast_to(normed[None], (4,) + normed.shape), "col", 0, 0, tiled=False
    )
    parts = [gathered.reshape(-1, width_row)] * 4

    mlp_preact = after(mlp_preact, normed)
    own_m = [
        (
            mlp_cotangent[start : start + size].astype(jnp.float32)
            * gelu_slope(mlp_preact[start : start + size].astype(jnp.float32))
        ).astype(jnp.bfloat16)
        for start, size in zip(STARTS, PIECES)
    ]
    side_m = [lax.ppermute(part, "row", CORE) for part in own_m]
    far_m = [lax.ppermute(part, "row", CHIP) for part in own_m]

    near_keep, near_send, mark = back(
        [
            [(0, qkv_cotangent), (tok_row, side_q)],
            [(start, part) for start, part in zip(STARTS, own_m)]
            + [(tok_row + start, part) for start, part in zip(STARTS, side_m)],
        ],
        [w_qkv, w_mlp],
        [tok_row, tok_row],
        jnp.bfloat16,
        order=order,
    )
    near_next = lax.ppermute(near_send, "col", NEXT)

    ready_q = after(far_q, near_send)
    farside_q = [
        lax.ppermute(ready_q[low : low + PART], "row", CORE) for low in range(0, tok_row, PART)
    ]
    places = jnp.stack([row_id ^ j for j in range(4)])
    takes_near = row_id // 2 == col_id // 2

    far, mark = back(
        [
            [(0, far_q)]
            + [(tok_row + place * PART, part) for place, part in enumerate(farside_q)]
        ],
        [w_qkv],
        [2 * tok_row],
        jnp.float32,
    )
    q_parts = [qkv_cotangent, side_q, far_q] + farside_q
    ready, farside_m, halves = [mark], [], []
    for index, turn in enumerate(TURNS):
        for k in turn:
            farside_m.append(lax.ppermute(after(far_m[k], *ready), "row", CORE))
        start, size = STARTS[turn[0]], sum(PIECES[k] for k in turn)
        keep, send, mark = back(
            [
                [(STARTS[k] - start, far_m[k]) for k in turn]
                + [(size + STARTS[k] - start, farside_m[k]) for k in turn]
            ],
            [w_mlp],
            [size, size],
            jnp.bfloat16,
            order=order,
            seed=far,
            seeds=((start, size), (tok_row + start, size)),
            hold=[mark],
            pin=False,
            tile=1536,
        )
        send = lax.ppermute(send, "col", NEXT)
        if index == 0:
            qkv_total, mark = weight_grad(places, parts, q_parts, tile=1152, hold=[mark])
            ready = [mark, send, near_next]
        halves.append((start, size, keep, send))

    all_m = own_m + side_m + far_m + farside_m
    mlp_total, mark = weight_grad(places, parts, all_m, tile=1024, high=1, hold=[mark])
    incoming = []
    for turn, (start, size, keep, send) in enumerate(halves):
        if turn == len(halves) - 1:
            keep, send = after((keep, send), mark, *[arrived for _, arrived in incoming])
        far_half = keep.astype(jnp.float32) + send.astype(jnp.float32)
        near_piece = near_keep[start : start + size].astype(jnp.float32)
        near_piece += near_next[start : start + size].astype(jnp.float32)
        own = jnp.where(takes_near, near_piece, far_half)
        other = jnp.where(takes_near, far_half, near_piece).astype(jnp.bfloat16)
        for low, high in SWAPS[turn]:
            incoming.append((own[low:high], lax.ppermute(other[low:high], "col", SKIP)))
    mlp_total, mark = weight_grad(
        places, parts, all_m, tile=1024, low=1, held=mlp_total, hold=[mark, other]
    )

    incoming = jnp.concatenate(
        [own + after(arrived, mark).astype(jnp.float32) for own, arrived in incoming], axis=0
    ) * scale_omega
    terms = row_sum_direct(
        jnp.stack([jnp.sum(incoming, axis=1), jnp.sum(incoming * xhat, axis=1)])
    ) / MODEL_WIDTH
    latent_input_gradient = rstd * (
        incoming - terms[0][:, None] - xhat * terms[1][:, None]
    )
    return latent_input_gradient.astype(jnp.bfloat16), qkv_total, mlp_total


def on_device(
    latents,
    modulation,
    sample_of,
    timestep,
    reward,
    qkv_cotangent,
    mlp_cotangent,
    mlp_preact,
    w_qkv,
    w_mlp,
):
    row_id = lax.axis_index("row")
    col_id = lax.axis_index("col")
    tok_col = latents.shape[0]
    tok_row = qkv_cotangent.shape[0]
    width_row = latents.shape[1]
    samples = reward.shape[0]
    sample_ids = jnp.arange(samples, dtype=jnp.int32)
    onehot = (sample_ids[:, None] == sample_of[None, :]).astype(jnp.float32)
    omega_sample = sample_weights(onehot, timestep, reward)
    omega_tokens = lookup(onehot, omega_sample[:, None])[:, 0]
    omega_rows = lax.dynamic_slice_in_dim(omega_tokens, row_id * tok_row, tok_row)[:, None]
    grad_q = (qkv_cotangent.astype(jnp.float32) * omega_rows).astype(jnp.bfloat16)
    grad_m = (
        mlp_cotangent.astype(jnp.float32) * gelu_slope(mlp_preact.astype(jnp.float32)) * omega_rows
    ).astype(jnp.bfloat16)
    mod_flat = modulation.reshape(samples, 2 * width_row)
    input_float_copy = latents.astype(jnp.float32)
    own_onehot = lax.dynamic_slice_in_dim(onehot, col_id * tok_col, tok_col, 1)
    own_mod = lookup(own_onehot, mod_flat)
    sample_offset = own_mod[:, :width_row]
    sample_scale_factor = 1.0 + own_mod[:, width_row:]
    total_sum, total_square = lax.psum(
        (jnp.sum(input_float_copy, axis=1), jnp.sum(input_float_copy * input_float_copy, axis=1)),
        "row",
    )
    feature_average = (total_sum / MODEL_WIDTH)[:, None]
    inverse_deviation = lax.rsqrt(
        (total_square / MODEL_WIDTH)[:, None] - feature_average * feature_average + EPS
    )
    centered_normalized = (input_float_copy - feature_average) * inverse_deviation
    norm_output = (centered_normalized * sample_scale_factor + sample_offset).astype(jnp.bfloat16)
    normed_all = lax.all_gather(norm_output, "col", axis=0, tiled=True)
    all_q, all_m = (
        lax.all_gather(grad_q, "row", axis=0, tiled=True),
        lax.all_gather(grad_m, "row", axis=0, tiled=True),
    )
    qkv_total = over_tokens(normed_all, all_q)
    mlp_total = over_tokens(normed_all, all_m)
    normed_grad = lax.psum_scatter(
        (against_weight(all_q, w_qkv) + against_weight(all_m, w_mlp)).astype(jnp.bfloat16),
        "col",
        scatter_dimension=0,
        tiled=True,
    ).astype(jnp.float32)
    incoming_gradient = normed_grad * sample_scale_factor
    first_moment_term, second_moment_term = lax.psum(
        (
            jnp.sum(incoming_gradient, axis=1),
            jnp.sum(incoming_gradient * centered_normalized, axis=1),
        ),
        "row",
    )
    latent_input_gradient = inverse_deviation * (
        incoming_gradient
        - (first_moment_term / MODEL_WIDTH)[:, None]
        - centered_normalized * (second_moment_term / MODEL_WIDTH)[:, None]
    )
    return (
        latent_input_gradient.astype(jnp.bfloat16),
        qkv_total.astype(jnp.bfloat16),
        mlp_total.astype(jnp.bfloat16),
    )


def solution(mesh):
    in_specs = (
        P(("groups", "col"), "row"),
        P("groups", None, "row"),
        P("groups"),
        P("groups"),
        P("groups"),
        P(("groups", "row"), "col"),
        P(("groups", "row"), "col"),
        P(("groups", "row"), "col"),
        P("row", "col"),
        P("row", "col"),
    )
    out_specs = (
        P(("groups", "col"), "row"),
        P(("groups", "row"), "col"),
        P(("groups", "row"), "col"),
    )
    small = mesh.shape["row"] == 4 and mesh.shape["col"] == 4
    return jax.shard_map(
        on_grid if small else on_device,
        mesh=mesh,
        in_specs=in_specs,
        out_specs=out_specs,
        check_vma=False,
    )
```

```python
import functools
import math

import jax
import jax.numpy as jnp
from jax import lax
from jax.experimental import pallas as pl
from jax.experimental.pallas import tpu as pltpu
from jax.sharding import PartitionSpec as P

MODEL_WIDTH = 3072
TSTEPS = 1000


EPS = 1e-06
ROOT = math.sqrt(2.0 / math.pi)
CUBE = 0.044715
VMEM_BYTES = 36 * 2**20
QUICK = pl.CostEstimate(flops=1, bytes_accessed=1, transcendentals=0)
MARK = jax.ShapeDtypeStruct((8, 128), jnp.float32)
AHEAD = 2

CORE = [(0, 1), (1, 0), (2, 3), (3, 2)]
CHIP = [(0, 2), (2, 0), (1, 3), (3, 1)]
BOTH = [(0, 3), (3, 0), (1, 2), (2, 1)]
NEXT, SKIP = CORE, CHIP
PIECES = (160, 96)
STARTS = tuple(sum(PIECES[:k]) for k in range(len(PIECES)))
TURNS = ((0,), (1,))
SWAPS = (((0, 112), (112, 160)), ((0, 96),))
PART = 128


def gelu_slope(value):
    inner = ROOT * (value + CUBE * value * value * value)
    tangent = jnp.tanh(inner)
    return 0.5 * (1.0 + tangent) + 0.5 * value * (1.0 - tangent * tangent) * ROOT * (
        1.0 + 3.0 * CUBE * value * value
    )


def over_tokens(left, right):
    return lax.dot_general(
        left, right, (((0,), (0,)), ((), ())), preferred_element_type=jnp.float32
    )


def against_weight(left, right):
    return lax.dot_general(
        left, right, (((1,), (1,)), ((), ())), preferred_element_type=jnp.float32
    )


def lookup(onehot, table):
    return lax.dot_general(
        onehot,
        table,
        (((0,), (0,)), ((), ())),
        precision=lax.Precision.HIGHEST,
        preferred_element_type=jnp.float32,
    )


def sample_weights(onehot, timestep, reward):
    counts = jnp.sum(onehot, axis=1)
    level = (timestep.astype(jnp.float32) + 0.5) / TSTEPS
    return reward * (0.5 + 1.5 * level * (2.0 - level)) * lax.rsqrt(counts)


def params(**more):
    return pltpu.CompilerParams(vmem_limit_bytes=VMEM_BYTES, **more)


def back_kernel(layout, tile, ordered, seeds, holds, *refs):
    refs = list(refs)
    order = refs.pop(0) if ordered else None
    lefts = [[(place, refs.pop(0)) for place in places] for places in layout]
    weights = [refs.pop(0) for _ in layout]
    seed = refs.pop(0) if seeds else None
    del refs[:holds]
    left_sem, weight_sem, seed_sem = refs[-3:]
    left_buf, weight_buf, total = refs[-6:-3]
    mark, outs = refs[-7], refs[:-7]
    mark[...] = jnp.zeros_like(mark)

    first, place = [], 0
    for index, (start, size) in enumerate(seeds):
        first.append(
            pltpu.make_async_copy(
                seed.at[pl.ds(start, size)], total.at[pl.ds(place, size)], seed_sem.at[index]
            )
        )
        place += size
    for copy in first:
        copy.start()
    tiles, column, number = [], 0, 0
    for group, weight in zip(lefts, weights):
        for low in range(0, weight.shape[1], tile):
            span = pl.ds(column, tile)
            copies = [
                pltpu.make_async_copy(
                    weight.at[:, pl.ds(low, tile)], weight_buf.at[:, span], weight_sem.at[column // tile]
                )
            ]
            for place, left in group:
                copies.append(
                    pltpu.make_async_copy(
                        left.at[:, pl.ds(low, tile)],
                        left_buf.at[pl.ds(place, left.shape[0]), span],
                        left_sem.at[number],
                    )
                )
                number += 1
            tiles.append((span, copies))
            column += tile
    start_tiles = lambda low, high: [copy.start() for _, copies in tiles[low:high] for copy in copies]
    start_tiles(0, AHEAD)
    for copy in first:
        copy.wait()
    for index, (span, copies) in enumerate(tiles):
        start_tiles(index + AHEAD, index + AHEAD + 1)
        for copy in copies:
            copy.wait()
        product = against_weight(left_buf[:, span], weight_buf[:, span])
        if index or seeds:
            total[...] += product
        else:
            total[...] = product
    place = 0
    for index, out in enumerate(outs):
        size = out.shape[0]
        if ordered:
            place = pl.multiple_of(order[index] * size, size)
        out[...] = total[pl.ds(place, size), :].astype(out.dtype)
        place += size


def back(groups, weights, sizes, dtype, tile=768, order=None, seed=None, seeds=(), hold=(), pin=True):
    width = weights[0].shape[0]
    rows = sum(sizes)
    depth = sum(weight.shape[1] for weight in weights)
    layout = [[place for place, _ in group] for group in groups]
    copies = sum(len(group) * (weight.shape[1] // tile) for group, weight in zip(groups, weights))
    operands = [left for group in groups for _, left in group]
    if pin:
        operands = [pltpu.with_memory_space_constraint(left, pltpu.HBM) for left in operands]
    operands += [pltpu.with_memory_space_constraint(weight, pltpu.HBM) for weight in weights]
    if seed is not None:
        operands.append(pltpu.with_memory_space_constraint(seed, pltpu.HBM))
    operands += list(hold)
    in_specs = [pl.BlockSpec(memory_space=pl.ANY)] * len(operands)
    if order is not None:
        operands.insert(0, order)
        in_specs.insert(0, pl.BlockSpec(memory_space=pltpu.SMEM))
    return pl.pallas_call(
        functools.partial(
            back_kernel, layout, tile, order is not None, seeds, len(hold)
        ),
        in_specs=in_specs,
        out_specs=[pl.BlockSpec(memory_space=pltpu.VMEM)] * (len(sizes) + 1),
        out_shape=[
            pltpu.HBM((size, width), dtype) if order is None else jax.ShapeDtypeStruct((size, width), dtype)
            for size in sizes
        ]
        + [MARK],
        scratch_shapes=[
            pltpu.VMEM((rows, depth), jnp.bfloat16),
            pltpu.VMEM((width, depth), jnp.bfloat16),
            pltpu.VMEM((rows, width), jnp.float32),
            pltpu.SemaphoreType.DMA((copies,)),
            pltpu.SemaphoreType.DMA((depth // tile,)),
            pltpu.SemaphoreType.DMA((max(1, len(seeds)),)),
        ],
        compiler_params=params(),
        cost_estimate=QUICK,
    )(*operands)


def weight_kernel(count, holds, places, *refs):
    parts, grads, (out, mark, normed) = refs[:4], refs[4 : 4 + count], refs[-3:]

    @pl.when(pl.program_id(0) == 0)
    def _():
        for index, part in enumerate(parts):
            size = part.shape[0]
            normed[pl.ds(pl.multiple_of(places[index] * size, size), size), :] = part[...]
        mark[...] = jnp.zeros_like(mark)

    joined = jnp.concatenate([grad[...] for grad in grads], axis=0)
    out[...] = over_tokens(normed[...], joined).astype(out.dtype)


def weight_grad(
    places, parts, grads, tile=768, low=0, high=None, held=None, hold=(), pin=True
):
    width = parts[0].shape[1]
    tokens = parts[0].shape[0]
    columns = grads[0].shape[1]
    high = columns // tile if high is None else high
    extra = list(hold) + ([] if held is None else [held])
    arrays = list(parts) + list(grads)
    if pin:
        arrays = [pltpu.with_memory_space_constraint(array, pltpu.HBM) for array in arrays]
    operands = [places] + arrays + extra
    return pl.pallas_call(
        functools.partial(weight_kernel, len(grads), len(extra)),
        grid=(high - low,),
        in_specs=[pl.BlockSpec(memory_space=pltpu.SMEM)]
        + [pl.BlockSpec((tokens // 4, width), lambda i, j=j: (j, 0)) for j in range(4)]
        + [pl.BlockSpec((grad.shape[0], tile), lambda i: (0, i + low)) for grad in grads]
        + [pl.BlockSpec(memory_space=pl.ANY)] * len(extra),
        out_specs=[
            pl.BlockSpec((width, tile), lambda i: (0, i + low)),
            pl.BlockSpec(MARK.shape, lambda i: (0, 0)),
        ],
        out_shape=[jax.ShapeDtypeStruct((width, columns), jnp.bfloat16), MARK],
        scratch_shapes=[pltpu.VMEM((tokens, width), jnp.bfloat16)],
        input_output_aliases={} if held is None else {len(operands) - 1: 0},
        compiler_params=params(),
        cost_estimate=QUICK,
    )(*operands)


def after(value, *others):
    return lax.optimization_barrier((value, others))[0]


def row_sum(pair):
    pair += lax.ppermute(pair, "row", CHIP)
    return pair + lax.ppermute(pair, "row", CORE)


def row_sum_direct(pair):
    return (
        pair
        + lax.ppermute(pair, "row", CORE)
        + lax.ppermute(pair, "row", CHIP)
        + lax.ppermute(pair, "row", BOTH)
    )


def on_grid(
    latents,
    modulation,
    sample_of,
    timestep,
    reward,
    qkv_cotangent,
    mlp_cotangent,
    mlp_preact,
    w_qkv,
    w_mlp,
):
    row_id = lax.axis_index("row")
    col_id = lax.axis_index("col")
    tok_col, width_row = latents.shape
    tok_row = qkv_cotangent.shape[0]
    samples = reward.shape[0]
    own_first = (row_id ^ col_id) % 2
    order = jnp.stack([own_first, 1 - own_first])

    latents32 = latents.astype(jnp.float32)
    moments = jnp.stack([jnp.sum(latents32, axis=1), jnp.sum(latents32 * latents32, axis=1)])
    far_q = lax.ppermute(after(qkv_cotangent, moments), "row", CHIP)
    moments = row_sum(moments)
    side_q = lax.ppermute(qkv_cotangent, "row", CORE)

    sample_ids = jnp.arange(samples, dtype=jnp.int32)[:, None]
    omega_sample = sample_weights(
        (sample_ids == sample_of[None, :]).astype(jnp.float32), timestep, reward
    )
    own_samples = lax.dynamic_slice_in_dim(sample_of, col_id * tok_col, tok_col)
    own_onehot = (sample_ids == own_samples[None, :]).astype(jnp.float32)
    own_mod = lookup(own_onehot, modulation.reshape(samples, 2 * width_row))
    own_omega = lookup(own_onehot, omega_sample[:, None])
    offset = own_mod[:, :width_row]
    scale = 1.0 + own_mod[:, width_row:]
    mean = (moments[0] / MODEL_WIDTH)[:, None]
    rstd = lax.rsqrt((moments[1] / MODEL_WIDTH)[:, None] - mean * mean + EPS)
    xhat = (latents32 - mean) * rstd
    normed = ((xhat * scale + offset) * own_omega).astype(jnp.bfloat16)
    scale_omega = scale * own_omega
    gathered = lax.all_to_all(
        jnp.broadcast_to(normed[None], (4,) + normed.shape), "col", 0, 0, tiled=False
    )
    parts = [gathered.reshape(-1, width_row)] * 4

    mlp_preact = after(mlp_preact, normed)
    own_m = [
        (
            mlp_cotangent[start : start + size].astype(jnp.float32)
            * gelu_slope(mlp_preact[start : start + size].astype(jnp.float32))
        ).astype(jnp.bfloat16)
        for start, size in zip(STARTS, PIECES)
    ]
    side_m = [lax.ppermute(part, "row", CORE) for part in own_m]
    far_m = [lax.ppermute(part, "row", CHIP) for part in own_m]

    near_keep, near_send, mark = back(
        [
            [(0, qkv_cotangent), (tok_row, side_q)],
            [(start, part) for start, part in zip(STARTS, own_m)]
            + [(tok_row + start, part) for start, part in zip(STARTS, side_m)],
        ],
        [w_qkv, w_mlp],
        [tok_row, tok_row],
        jnp.bfloat16,
        order=order,
    )
    near_next = lax.ppermute(near_send, "col", NEXT)

    ready_q = after(far_q, near_send)
    farside_q = [
        lax.ppermute(ready_q[low : low + PART], "row", CORE) for low in range(0, tok_row, PART)
    ]
    places = jnp.stack([row_id ^ j for j in range(4)])
    takes_near = row_id // 2 == col_id // 2

    far, mark = back(
        [
            [(0, far_q)]
            + [(tok_row + place * PART, part) for place, part in enumerate(farside_q)]
        ],
        [w_qkv],
        [2 * tok_row],
        jnp.float32,
    )
    q_parts = [qkv_cotangent, side_q, far_q] + farside_q
    ready, farside_m, halves = [mark], [], []
    for index, turn in enumerate(TURNS):
        for k in turn:
            farside_m.append(lax.ppermute(after(far_m[k], *ready), "row", CORE))
        start, size = STARTS[turn[0]], sum(PIECES[k] for k in turn)
        keep, send, mark = back(
            [
                [(STARTS[k] - start, far_m[k]) for k in turn]
                + [(size + STARTS[k] - start, farside_m[k]) for k in turn]
            ],
            [w_mlp],
            [size, size],
            jnp.bfloat16,
            order=order,
            seed=far,
            seeds=((start, size), (tok_row + start, size)),
            hold=[mark],
            pin=False,
            tile=1536,
        )
        send = lax.ppermute(send, "col", NEXT)
        if index == 0:
            qkv_total, mark = weight_grad(places, parts, q_parts, tile=1152, hold=[mark])
            ready = [mark, send, near_next]
        halves.append((start, size, keep, send))

    all_m = own_m + side_m + far_m + farside_m
    mlp_total, mark = weight_grad(places, parts, all_m, tile=1024, high=1, hold=[mark])
    incoming = []
    for turn, (start, size, keep, send) in enumerate(halves):
        if turn == len(halves) - 1:
            keep, send = after((keep, send), mark, *[arrived for _, arrived in incoming])
        far_half = keep.astype(jnp.float32) + send.astype(jnp.float32)
        near_piece = near_keep[start : start + size].astype(jnp.float32)
        near_piece += near_next[start : start + size].astype(jnp.float32)
        own = jnp.where(takes_near, near_piece, far_half)
        other = jnp.where(takes_near, far_half, near_piece).astype(jnp.bfloat16)
        for low, high in SWAPS[turn]:
            incoming.append((own[low:high], lax.ppermute(other[low:high], "col", SKIP)))
    mlp_total, mark = weight_grad(
        places, parts, all_m, tile=1024, low=1, held=mlp_total, hold=[mark, other]
    )

    incoming = jnp.concatenate(
        [own + after(arrived, mark).astype(jnp.float32) for own, arrived in incoming], axis=0
    ) * scale_omega
    terms = row_sum_direct(
        jnp.stack([jnp.sum(incoming, axis=1), jnp.sum(incoming * xhat, axis=1)])
    ) / MODEL_WIDTH
    latent_input_gradient = rstd * (
        incoming - terms[0][:, None] - xhat * terms[1][:, None]
    )
    return latent_input_gradient.astype(jnp.bfloat16), qkv_total, mlp_total


def on_device(
    latents,
    modulation,
    sample_of,
    timestep,
    reward,
    qkv_cotangent,
    mlp_cotangent,
    mlp_preact,
    w_qkv,
    w_mlp,
):
    row_id = lax.axis_index("row")
    col_id = lax.axis_index("col")
    tok_col = latents.shape[0]
    tok_row = qkv_cotangent.shape[0]
    width_row = latents.shape[1]
    samples = reward.shape[0]
    sample_ids = jnp.arange(samples, dtype=jnp.int32)
    onehot = (sample_ids[:, None] == sample_of[None, :]).astype(jnp.float32)
    omega_sample = sample_weights(onehot, timestep, reward)
    omega_tokens = lookup(onehot, omega_sample[:, None])[:, 0]
    omega_rows = lax.dynamic_slice_in_dim(omega_tokens, row_id * tok_row, tok_row)[:, None]
    grad_q = (qkv_cotangent.astype(jnp.float32) * omega_rows).astype(jnp.bfloat16)
    grad_m = (
        mlp_cotangent.astype(jnp.float32) * gelu_slope(mlp_preact.astype(jnp.float32)) * omega_rows
    ).astype(jnp.bfloat16)
    mod_flat = modulation.reshape(samples, 2 * width_row)
    input_float_copy = latents.astype(jnp.float32)
    own_onehot = lax.dynamic_slice_in_dim(onehot, col_id * tok_col, tok_col, 1)
    own_mod = lookup(own_onehot, mod_flat)
    sample_offset = own_mod[:, :width_row]
    sample_scale_factor = 1.0 + own_mod[:, width_row:]
    total_sum, total_square = lax.psum(
        (jnp.sum(input_float_copy, axis=1), jnp.sum(input_float_copy * input_float_copy, axis=1)),
        "row",
    )
    feature_average = (total_sum / MODEL_WIDTH)[:, None]
    inverse_deviation = lax.rsqrt(
        (total_square / MODEL_WIDTH)[:, None] - feature_average * feature_average + EPS
    )
    centered_normalized = (input_float_copy - feature_average) * inverse_deviation
    norm_output = (centered_normalized * sample_scale_factor + sample_offset).astype(jnp.bfloat16)
    normed_all = lax.all_gather(norm_output, "col", axis=0, tiled=True)
    all_q, all_m = (
        lax.all_gather(grad_q, "row", axis=0, tiled=True),
        lax.all_gather(grad_m, "row", axis=0, tiled=True),
    )
    qkv_total = over_tokens(normed_all, all_q)
    mlp_total = over_tokens(normed_all, all_m)
    normed_grad = lax.psum_scatter(
        (against_weight(all_q, w_qkv) + against_weight(all_m, w_mlp)).astype(jnp.bfloat16),
        "col",
        scatter_dimension=0,
        tiled=True,
    ).astype(jnp.float32)
    incoming_gradient = normed_grad * sample_scale_factor
    first_moment_term, second_moment_term = lax.psum(
        (
            jnp.sum(incoming_gradient, axis=1),
            jnp.sum(incoming_gradient * centered_normalized, axis=1),
        ),
        "row",
    )
    latent_input_gradient = inverse_deviation * (
        incoming_gradient
        - (first_moment_term / MODEL_WIDTH)[:, None]
        - centered_normalized * (second_moment_term / MODEL_WIDTH)[:, None]
    )
    return (
        latent_input_gradient.astype(jnp.bfloat16),
        qkv_total.astype(jnp.bfloat16),
        mlp_total.astype(jnp.bfloat16),
    )


def solution(mesh):
    in_specs = (
        P(("groups", "col"), "row"),
        P("groups", None, "row"),
        P("groups"),
        P("groups"),
        P("groups"),
        P(("groups", "row"), "col"),
        P(("groups", "row"), "col"),
        P(("groups", "row"), "col"),
        P("row", "col"),
        P("row", "col"),
    )
    out_specs = (
        P(("groups", "col"), "row"),
        P(("groups", "row"), "col"),
        P(("groups", "row"), "col"),
    )
    small = mesh.shape["row"] == 4 and mesh.shape["col"] == 4
    return jax.shard_map(
        on_grid if small else on_device,
        mesh=mesh,
        in_specs=in_specs,
        out_specs=out_specs,
        check_vma=False,
    )
```
